768 devices in a mesh: dp: 4 (over x), ctx: 6 (over z_hi, core), exp: 32 (over y, z_lo).
Axes of the slice: x: 4, y: 8, z: 12 (z_hi: 3, z_lo: 4; z = z_hi * 4 + z_lo), core: 2. Of those that a mesh axis runs over, the one named last changes fastest.
Arguments:
- queries: bfloat16 [4, 768, 128, 576], P('dp', 'ctx', 'exp'), may hold values from -7 to 7
- out_grad: bfloat16 [4, 768, 128, 512], P('dp', 'ctx', 'exp'), may hold values from -6 to 6
- latent_keys: bfloat16 [4, 768, 576], P('dp', 'ctx'), may hold values from -9 to 9
- kv_gain: float32 [512], replicated, may hold values from 0.5 to 2
- query_groups: int32 [4, 6], P('dp'), may hold values from 0 to 5, each once within a row
Outputs:
- grad_queries: bfloat16 [4, 768, 128, 576], P('dp', 'ctx', 'exp')
- grad_keys: float32 [4, 6, 128, 576], P('dp', 'ctx', 'exp')
- grad_gain: float32 [512], replicated
The draws below stay inside these ranges and needn't reach their ends.
Inputs may be any that keep to these rules, and one draw needn't show every extreme that they name: `query_groups`: each row names each group index once.
All inputs are finite; a program needn't handle non-finite values.
Results may differ from the reference program's by a relative error of at most 0.0049.
Values may be sent and summed in bfloat16 or wider, within the bound.
A program may use at most 32 MiB of HBM per device.

```python
import math
import jax
import jax.numpy as jnp
from jax import lax

LATENT = 512
ROPE = 64
GROUP = 128
HEADS = 128
BATCH = 4
QUERIES = 768
KEYS = 768
N_CTX = 6


def key_table(key, scale_low, scale_high, gap_size):
    key_width = LATENT + ROPE
    shape = (BATCH, KEYS, key_width)
    normal_part = jnp.clip(jax.random.normal(jax.random.fold_in(key, 1), shape, jnp.float32), -4.0, 4.0)
    key_rows = normal_part
    row_scale = jnp.exp(jax.random.uniform(jax.random.fold_in(key, 3), (BATCH, KEYS, 1), jnp.float32, math.log(scale_low), math.log(scale_high)))
    row_ids = jnp.arange(KEYS)[None, :, None]
    key_rows = jnp.where(row_ids < 2, key_rows, key_rows * row_scale)
    column_ids = jnp.arange(key_width)[None, None, :]
    first_row = key_rows[:, 0:1, :]
    lead_row = jnp.where(column_ids < 8, 1.0, first_row)
    twin_row = jnp.where(column_ids < 8, 1.0 - gap_size, first_row)
    key_rows = jnp.where(row_ids == 0, lead_row, jnp.where(row_ids == 1, twin_row, key_rows))
    return key_rows


def draw_latent_keys(key, part):
    key_rows = key_table(key, 1.0, 1.0, 0.74)
    return key_rows.astype(jnp.bfloat16)


def draw_queries(key, part):
    key = jax.random.fold_in(key, 5)
    full_shape = (BATCH, QUERIES, HEADS, LATENT + ROPE)
    values_drawn = jnp.clip(jax.random.normal(jax.random.fold_in(key, 1), full_shape, jnp.float32), -4.0, 4.0) * 0.3
    return values_drawn.astype(jnp.bfloat16)


def block_levels(rng, shape, cuts, smallest, top_value):
    level = 1.0
    for dim, parts in cuts:
        draws = jax.random.uniform(jax.random.fold_in(jax.random.fold_in(rng, 6), dim), (parts,), jnp.float32, smallest / len(cuts), top_value / len(cuts))
        level = level * jnp.repeat(jnp.exp(draws), shape[dim] // parts).reshape((-1,) + (1,) * (len(shape) - 1 - dim))
    return level


def bell_draw(key, dims, scale, limit, split=(), kind=jnp.bfloat16):
    factor_of = block_levels(key, dims, split, -0.22, 0.18) if split else 1.0
    array = jax.random.normal(key, dims, jnp.float32) * scale * factor_of
    return jnp.minimum(jnp.maximum(array, -limit), limit).astype(kind)


def setup_inputs(seed: int = 0) -> dict:
    seeds = jax.random.split(jax.random.key(seed), 6)
    return {
        "queries": draw_queries(jax.random.fold_in(seeds[5], 71), 0),
        "out_grad": bell_draw(seeds[1], (BATCH, QUERIES, HEADS, LATENT), 1.0, 6.0, ((0, 4), (1, 6), (2, 32))),
        "latent_keys": draw_latent_keys(jax.random.fold_in(seeds[5], 71), 0),
        "kv_gain": jnp.clip(jnp.exp(jax.random.uniform(seeds[3], (LATENT,), jnp.float32, math.log(0.5), math.log(2.0))), 0.5, 2.0),
        "query_groups": jax.vmap(lambda own: jax.random.permutation(own, N_CTX))(jax.random.split(seeds[4], BATCH)).reshape((BATCH, N_CTX)).astype(jnp.int32),
    }


SOFTMAX_SCALE = (0.1 * math.log(40.0) + 1.0) ** 2 / math.sqrt(192.0)
MASKED_SCORE = -1e+30

def one_sequence(queries, out_grad, latent_keys, visible):
    key_width = LATENT + ROPE
    values = latent_keys[:, :LATENT]

    def one_head(running, inputs):
        query_rows, grad_rows = inputs
        scores = jnp.dot(query_rows, latent_keys.T, preferred_element_type=jnp.float32) * SOFTMAX_SCALE
        scores = jnp.where(visible, scores, MASKED_SCORE)
        row_max = lax.optimization_barrier(jnp.max(scores, axis=1))
        exponent = jnp.where(visible, jnp.exp(scores - row_max[:, None]), 0.0)
        weights = exponent / lax.optimization_barrier(jnp.sum(exponent, axis=1))[:, None]
        grad_prob = jnp.dot(grad_rows, values.T, preferred_element_type=jnp.float32)
        row_delta = lax.optimization_barrier(jnp.sum(weights * grad_prob, axis=1))
        dscore = (weights * (grad_prob - row_delta[:, None])).astype(jnp.bfloat16)
        weights_low = weights.astype(jnp.bfloat16)
        grad_query = (jnp.dot(dscore, latent_keys, preferred_element_type=jnp.float32) * SOFTMAX_SCALE).astype(jnp.bfloat16)
        key_part = jnp.dot(dscore.T, query_rows, preferred_element_type=jnp.float32) * SOFTMAX_SCALE
        value_part = jnp.dot(weights_low.T, grad_rows, preferred_element_type=jnp.float32)
        key_part = key_part + jnp.pad(value_part, ((0, 0), (0, ROPE)))
        return (running + key_part, grad_query)
    initial = jnp.zeros((KEYS, key_width), jnp.float32)
    grad_keys, grad_heads = lax.scan(one_head, initial, (jnp.swapaxes(queries, 0, 1), jnp.swapaxes(out_grad, 0, 1)))
    return (jnp.swapaxes(grad_heads, 0, 1), grad_keys)

def reference(queries, out_grad, latent_keys, kv_gain, query_groups):
    key_width = LATENT + ROPE
    offsets = jnp.arange(GROUP, dtype=jnp.int32)
    key_pos = jnp.arange(KEYS, dtype=jnp.int32)

    def per_sequence(inputs):
        group_row = inputs[3].astype(jnp.int32)
        query_pos = (group_row[:, None] * GROUP + offsets[None, :]).reshape(-1)
        visible = key_pos[None, :] <= query_pos[:, None]
        return one_sequence(inputs[0], inputs[1], inputs[2], visible)
    grad_queries, grad_keys = lax.map(per_sequence, (queries, out_grad, latent_keys, query_groups))
    products = grad_keys[:, :, :LATENT] * latent_keys[:, :, :LATENT].astype(jnp.float32)
    grad_gain = lax.optimization_barrier(jnp.sum(products, axis=(0, 1))) / kv_gain
    return (grad_queries, grad_keys.reshape(BATCH, N_CTX, GROUP, key_width), grad_gain)
```

```python
import math

import jax
import jax.numpy as jnp
from jax import lax
from jax.experimental import pallas as pl
from jax.experimental.pallas import tpu as pltpu
from jax.sharding import PartitionSpec as P

LATENT = 512
WIDTH = 576
ROPE = WIDTH - LATENT
SCALE = (0.1 * math.log(40.0) + 1.0) ** 2 / math.sqrt(192.0)
MASKED = -1e30
MESH_ID = pl.DeviceIdType.MESH
F32 = jnp.float32
BF16 = jnp.bfloat16

X, Y, ZH, ZL, CORES = 4, 8, 3, 4, 2
QUARTER = WIDTH // 4
PIECES = ((0, 80), (80, 64))
Y_PEERS = (4, 3, 5, 2, 6, 1, 7)
Z_PEERS = tuple((rel, d) for rel in (1, 2, 0) for d in range(ZL) if (rel, d) != (0, 0))
X_PEERS = ((0, 1), (1, 0), (3, 0), (2, 0), (1, 1), (3, 1), (2, 1))
COLS_Y = 384
NT = (((1,), (1,)), ((), ()))
NN = (((1,), (0,)), ((), ()))


def dot(a, b, dims=NN):
    return lax.dot_general(a, b, dims, preferred_element_type=F32)


def kernel(
    q_hbm, do_hbm, kt_hbm, gain_ref, groups_ref,
    gq_hbm, gk_ref, gg_ref,
    qp, do_raw, do_f32, dop, kt, kr, st, dpt, ds, pw,
    stat, stat_in, h1, h2, h1_in, h2_in, t1, h1b, h1b_in, t2, t2_in,
    ga, ga_in, gb, gb_in, gc, gc_in, dq, dq_in, gq,
    local_sem, send_sem, recv_sem,
):
    x = lax.axis_index("dp")
    ctx = lax.axis_index("ctx")
    exp = lax.axis_index("exp")
    zh, core = ctx // CORES, ctx % CORES
    y, zl = exp // ZL, exp % ZL

    def device(dx=0, dy=0, dh=0, dl=0, dc=0):
        return (
            (x + dx) % X,
            ((zh + dh) % ZH) * CORES + (core + dc) % CORES,
            ((y + dy) % Y) * ZL + (zl + dl) % ZL,
        )

    count = [0]

    def remote(src, dst, **where):
        i = count[0]
        count[0] += 1
        return pltpu.make_async_remote_copy(
            src_ref=src, dst_ref=dst, send_sem=send_sem.at[i], recv_sem=recv_sem.at[i],
            device_id=device(**where), device_id_type=MESH_ID,
        )

    loads = [pltpu.make_async_copy(kt_hbm, kt.at[0], local_sem.at[0])]
    loads.append(pltpu.make_async_copy(do_hbm, do_raw, local_sem.at[1]))
    for h in range(4):
        loads.append(
            pltpu.make_async_copy(
                q_hbm.at[h], qp.at[h // 2, :, pl.ds((h % 2) * 128, 128)], local_sem.at[2 + h]
            )
        )
    for copy in loads:
        copy.start()

    barrier = pltpu.get_barrier_semaphore()
    peers = [dict(dh=rel, dl=d) for rel, d in Z_PEERS]
    peers += [dict(dy=d) for d in Y_PEERS]
    peers += [dict(dx=d, dc=c) for d, c in X_PEERS]
    for peer in peers:
        pl.semaphore_signal(barrier, inc=1, device_id=device(**peer), device_id_type=MESH_ID)
    loads[0].wait()
    pl.semaphore_wait(barrier, len(peers))

    p0 = (y % 4) * QUARTER
    first = {}
    for at, (off, rows) in enumerate(PIECES):
        for rel in (1, 2):
            part = pl.ds(pl.multiple_of(p0 + off, 16), rows)
            first[rel, at] = remote(kt.at[0, part], kt.at[rel, part], dh=ZH - rel)
            first[rel, at].start()

    for copy in loads[2:]:
        copy.wait()
    swap_q = remote(qp.at[pl.ds(0, 2)], qp.at[pl.ds(2, 2)], dc=1)
    swap_q.start()
    loads[1].wait()
    do_f32[...] = do_raw[...].astype(F32)
    for h in range(4):
        dop[h // 2, pl.ds((h % 2) * 128, 128), :] = do_f32[:, h, :].astype(BF16)
    swap_do = remote(dop.at[pl.ds(0, 2)], dop.at[pl.ds(2, 2)], dc=1)
    swap_do.start()

    second = []
    for at, (off, rows) in enumerate(PIECES):
        for rel in (1, 2):
            first[rel, at].wait_recv()
            part = pl.ds(pl.multiple_of(p0 + off, 16), rows)
            for dy in (1, Y - 1, 2 if at == 0 else Y - 2):
                copy = remote(kt.at[rel, part], kt.at[rel, part], dy=dy)
                copy.start()
                second.append(copy)

    swap_q.wait_recv()
    swap_do.wait_recv()

    def keys_in(rel):
        for c in range(0, LATENT, 128):
            kr[rel, :, c : c + 128] = kt[rel, c : c + 128, :].astype(F32).T.astype(BF16)
        kr[rel, :, LATENT:] = kt[rel, LATENT:, :].astype(F32).T.astype(BF16)

    diff = lax.broadcasted_iota(jnp.int32, (128, 256), 0) - (
        lax.broadcasted_iota(jnp.int32, (128, 256), 1) & 127
    )
    group = (groups_ref[0, ctx], groups_ref[0, zh * CORES + 1 - core])

    def score(rel):
        base = ((zh + rel) % ZH) * CORES + core
        keys = kr[rel]
        for cc in range(4):
            visible = diff <= (group[cc // 2] - base) * 128
            s = dot(keys, qp[cc]) * SCALE
            st[cc, pl.ds(rel * 128, 128), :] = jnp.where(visible, s, MASKED)
            dpt[cc, pl.ds(rel * 128, 128), :] = dot(keys[:, :LATENT], dop[cc], NT)

    keys_in(0)
    score(0)
    for copy in second:
        copy.wait_recv()
    for rel in (1, 2):
        keys_in(rel)
        score(rel)

    for cc in range(4):
        s = st[cc]
        m = jnp.max(s, axis=0, keepdims=True)
        p = jnp.where(s > 0.5 * MASKED, jnp.exp(s - m), 0.0)
        st[cc] = p
        stat[cc, 0:1, :] = m
        stat[cc, 1:2, :] = jnp.sum(p, axis=0, keepdims=True)
        stat[cc, 2:3, :] = jnp.sum(p * dpt[cc], axis=0, keepdims=True)
        stat[cc, 3:8, :] = jnp.zeros((5, 256), F32)
    swap_stat = remote(stat, stat_in, dc=1)
    swap_stat.start()
    swap_stat.wait_recv()

    for cc in range(4):
        other = (cc + 2) % 4
        m0, l0, w0 = stat[cc, 0:1, :], stat[cc, 1:2, :], stat[cc, 2:3, :]
        m1, l1, w1 = stat_in[other, 0:1, :], stat_in[other, 1:2, :], stat_in[other, 2:3, :]
        m = jnp.maximum(m0, m1)
        e0, e1 = jnp.exp(m0 - m), jnp.exp(m1 - m)
        inv = 1.0 / (l0 * e0 + l1 * e1)
        delta = (w0 * e0 + w1 * e1) * inv
        w = st[cc] * (e0 * inv)
        pw[cc] = w.astype(BF16)
        ds[cc] = (w * (dpt[cc] - delta)).astype(BF16)

    out_row = lax.broadcasted_iota(jnp.int32, (128, 128), 0)
    in_row = lax.broadcasted_iota(jnp.int32, (128, 128), 1)
    wanted = ((out_row & 31) >> 2) * 16 + (out_row >> 5) * 4 + (out_row & 3)
    by_z = (in_row == wanted).astype(BF16)
    gain = jnp.zeros((1, LATENT), F32)
    for rel in range(3):
        rows = pl.ds(rel * 128, 128)
        dk = dot(ds[0, rows, :], qp[0], NT)
        dv = dot(pw[0, rows, :], dop[0])
        for cc in range(1, 4):
            dk = dk + dot(ds[cc, rows, :], qp[cc], NT)
            dv = dv + dot(pw[cc, rows, :], dop[cc])
        dk = dk * SCALE
        full = dk[:, :LATENT] + dv
        gain = gain + jnp.sum(full * kr[rel, :, :LATENT].astype(F32), axis=0, keepdims=True)
        h1[rel] = full[:, :COLS_Y].astype(BF16)
        h2[rel, :, 0:128] = dot(by_z, full[:, COLS_Y:].astype(BF16)).astype(BF16)
        h2[rel, :, 128 : 128 + ROPE] = dot(by_z, dk[:, LATENT:].astype(BF16)).astype(BF16)
        h2[rel, :, 128 + ROPE :] = jnp.zeros((128, 128 - ROPE), BF16)

    def pack(row, ref):
        for t in range(4):
            ref[t : t + 1, :] = row[:, t * 128 : (t + 1) * 128]
        ref[4:8, :] = jnp.zeros((4, 128), F32)

    pack(gain, ga)
    gain_a = [remote(ga, ga_in.at[i], dx=d, dc=c) for i, (d, c) in enumerate(X_PEERS)]
    for copy in gain_a:
        copy.start()

    def y_rows(dy):
        return pl.ds(pl.multiple_of(((y + dy) % Y) * 16, 16), 16)

    def z_rows(dl):
        return pl.ds(pl.multiple_of(((zl + dl) % ZL) * 32, 32), 32)

    stage_y = [remote(h1.at[:, y_rows(d), :], h1_in.at[i], dy=d) for i, d in enumerate(Y_PEERS)]
    stage_z = [
        remote(h2.at[rel, z_rows(d), :], h2_in.at[i], dh=rel, dl=d)
        for i, (rel, d) in enumerate(Z_PEERS)
    ]
    for i in range(len(Z_PEERS)):
        stage_z[i].start()
        if i < len(Y_PEERS):
            stage_y[i].start()

    def query_part(cc):
        total = dot(kt[0], ds[cc, 0:128, :])
        for rel in (1, 2):
            total = total + dot(kt[rel], ds[cc, rel * 128 : rel * 128 + 128, :])
        return total * SCALE

    swap_dq = []
    for cc in (2, 3):
        dq[cc - 2] = query_part(cc)
        copy = remote(dq.at[cc - 2], dq_in.at[cc - 2], dc=1)
        copy.start()
        swap_dq.append(copy)

    for copy in gain_a:
        copy.wait_recv()
    total = ga[...]
    for i in range(len(X_PEERS)):
        total = total + ga_in[i]
    gb[...] = total
    gain_b = [remote(gb, gb_in.at[i], dy=d) for i, d in enumerate(Y_PEERS)]
    for copy in gain_b:
        copy.start()

    stores = []
    for cc in range(2):
        own = query_part(cc)
        swap_dq[cc].wait_recv()
        gq[cc] = (own + dq_in[cc]).astype(BF16)
        for h in range(2):
            store = pltpu.make_async_copy(
                gq.at[cc, :, pl.ds(h * 128, 128)], gq_hbm.at[cc * 2 + h],
                local_sem.at[6 + cc * 2 + h],
            )
            store.start()
            stores.append(store)

    t1[...] = jnp.zeros_like(t1)
    for copy in stage_y:
        copy.wait_recv()
    for rel in range(3):
        part = h1[rel, y_rows(0), :].astype(F32)
        for i in range(len(Y_PEERS)):
            part = part + h1_in[i, rel].astype(F32)
        for l in range(ZL):
            for t in range(3):
                t1[rel, l, t * 4 : t * 4 + 4, :] = part[l * 4 : l * 4 + 4, t * 128 : (t + 1) * 128]
    h1b[...] = t1[...].astype(BF16)
    stage_yz = [
        remote(h1b.at[rel, (zl + d) % ZL], h1b_in.at[i], dh=rel, dl=d)
        for i, (rel, d) in enumerate(Z_PEERS)
    ]
    for copy in stage_yz:
        copy.start()

    for copy in stage_z:
        copy.wait_recv()
    part = h2[0, z_rows(0), :].astype(F32)
    for i in range(len(Z_PEERS)):
        part = part + h2_in[i].astype(F32)
    for yy in range(Y):
        for t in range(2):
            t2[yy, t * 4 : t * 4 + 4, :] = part[yy * 4 : yy * 4 + 4, t * 128 : (t + 1) * 128]
    stage_zy = [remote(t2.at[(y + d) % Y], t2_in.at[i], dy=d) for i, d in enumerate(Y_PEERS)]
    for copy in stage_zy:
        copy.start()

    for copy in gain_b:
        copy.wait_recv()
    total = gb[...]
    for i in range(len(Y_PEERS)):
        total = total + gb_in[i]
    gc[...] = total
    gain_c = [remote(gc, gc_in.at[i], dh=rel, dl=d) for i, (rel, d) in enumerate(Z_PEERS)]
    for copy in gain_c:
        copy.start()

    for copy in stage_yz:
        copy.wait_recv()
    part = t1[0, zl]
    for i in range(len(Z_PEERS)):
        part = part + h1b_in[i].astype(F32)
    for t in range(3):
        gk_ref[:, t * 128 : (t + 1) * 128] = part[t * 4 : t * 4 + 4, :]
    for copy in stage_zy:
        copy.wait_recv()
    part = t2[y]
    for i in range(len(Y_PEERS)):
        part = part + t2_in[i]
    gk_ref[:, COLS_Y:LATENT] = part[0:4, :]
    gk_ref[:, LATENT:] = part[4:8, :ROPE]
    for copy in gain_c:
        copy.wait_recv()
    total = gc[...]
    for i in range(len(Z_PEERS)):
        total = total + gc_in[i]
    gg_ref[...] = total[0:4, :] / gain_ref[...]

    for copy in stores:
        copy.wait()
    sent = list(first.values()) + second + [swap_q, swap_do, swap_stat] + swap_dq
    sent += gain_a + gain_b + gain_c + stage_y + stage_z + stage_yz + stage_zy
    for copy in sent:
        copy.wait_send()


N_COPIES = 4 + 12 + 3 + 2 + len(X_PEERS) + 3 * len(Y_PEERS) + 3 * len(Z_PEERS)


def body(queries, out_grad, latent_keys, kv_gain, query_groups):
    q_t = jnp.transpose(queries[0], (1, 2, 0))
    k_t = jnp.transpose(latent_keys[0], (1, 0))
    any_spec = pl.BlockSpec(memory_space=pl.ANY)
    vmem_spec = pl.BlockSpec(memory_space=pltpu.VMEM)
    ny, nz, nx = len(Y_PEERS), len(Z_PEERS), len(X_PEERS)
    gq, gk, gg = pl.pallas_call(
        kernel,
        out_shape=(
            jax.ShapeDtypeStruct((4, WIDTH, 128), BF16),
            jax.ShapeDtypeStruct((4, WIDTH), F32),
            jax.ShapeDtypeStruct((4, 128), F32),
        ),
        in_specs=[any_spec, any_spec, any_spec, vmem_spec, pl.BlockSpec(memory_space=pltpu.SMEM)],
        out_specs=(any_spec, vmem_spec, vmem_spec),
        scratch_shapes=[
            pltpu.VMEM((4, WIDTH, 256), BF16),
            pltpu.VMEM((128, 4, LATENT), BF16),
            pltpu.VMEM((128, 4, LATENT), F32),
            pltpu.VMEM((4, 256, LATENT), BF16),
            pltpu.VMEM((3, WIDTH, 128), BF16),
            pltpu.VMEM((3, 128, WIDTH), BF16),
            pltpu.VMEM((4, 384, 256), F32),
            pltpu.VMEM((4, 384, 256), F32),
            pltpu.VMEM((4, 384, 256), BF16),
            pltpu.VMEM((4, 384, 256), BF16),
            pltpu.VMEM((4, 8, 256), F32),
            pltpu.VMEM((4, 8, 256), F32),
            pltpu.VMEM((3, 128, COLS_Y), BF16),
            pltpu.VMEM((3, 128, 256), BF16),
            pltpu.VMEM((ny, 3, 16, COLS_Y), BF16),
            pltpu.VMEM((nz, 32, 256), BF16),
            pltpu.VMEM((3, ZL, 16, 128), F32),
            pltpu.VMEM((3, ZL, 16, 128), BF16),
            pltpu.VMEM((nz, 16, 128), BF16),
            pltpu.VMEM((Y, 8, 128), F32),
            pltpu.VMEM((ny, 8, 128), F32),
            pltpu.VMEM((8, 128), F32),
            pltpu.VMEM((nx, 8, 128), F32),
            pltpu.VMEM((8, 128), F32),
            pltpu.VMEM((ny, 8, 128), F32),
            pltpu.VMEM((8, 128), F32),
            pltpu.VMEM((nz, 8, 128), F32),
            pltpu.VMEM((2, WIDTH, 256), F32),
            pltpu.VMEM((2, WIDTH, 256), F32),
            pltpu.VMEM((2, WIDTH, 256), BF16),
            pltpu.SemaphoreType.DMA((10,)),
            pltpu.SemaphoreType.DMA((N_COPIES,)),
            pltpu.SemaphoreType.DMA((N_COPIES,)),
        ],
        compiler_params=pltpu.CompilerParams(
            collective_id=0, has_side_effects=True, vmem_limit_bytes=48 * 2**20
        ),
        cost_estimate=pl.CostEstimate(
            flops=5 * 2 * 512 * 768 * 550, bytes_accessed=3 * 2**20, transcendentals=512 * 768
        ),
        name="mla_backward",
    )(q_t, out_grad[0], k_t, kv_gain.reshape(4, 128), query_groups)
    grad_queries = jnp.transpose(gq, (2, 0, 1))[None]
    return grad_queries, gk.reshape(1, 1, 4, WIDTH), gg.reshape(LATENT)


def solution(mesh):
    in_specs = (
        P("dp", "ctx", "exp", None),
        P("dp", "ctx", "exp", None),
        P("dp", "ctx", None),
        P(),
        P("dp", None),
    )
    out_specs = (P("dp", "ctx", "exp", None), P("dp", "ctx", "exp", None), P())
    return jax.shard_map(body, mesh=mesh, in_specs=in_specs, out_specs=out_specs, check_vma=False)
```

```python
import math

import jax
import jax.numpy as jnp
from jax import lax
from jax.experimental import pallas as pl
from jax.experimental.pallas import tpu as pltpu
from jax.sharding import PartitionSpec as P

LATENT = 512
WIDTH = 576
ROPE = WIDTH - LATENT
SCALE = (0.1 * math.log(40.0) + 1.0) ** 2 / math.sqrt(192.0)
MASKED = -1e30
MESH_ID = pl.DeviceIdType.MESH
F32 = jnp.float32
BF16 = jnp.bfloat16

X, Y, ZH, ZL, CORES = 4, 8, 3, 4, 2
QUARTER = WIDTH // 4
PIECES = ((0, 80), (80, 64))
Y_PEERS = (4, 3, 5, 2, 6, 1, 7)
Z_PEERS = (6, 5, 7, 4, 8, 3, 9, 2, 10, 1, 11)
Z_FAR = 5
X_PEERS = ((0, 1), (1, 0), (3, 0), (2, 0), (1, 1), (3, 1), (2, 1))
COLS_Y = 384
NT = (((1,), (1,)), ((), ()))
NN = (((1,), (0,)), ((), ()))


def dot(a, b, dims=NN):
    return lax.dot_general(a, b, dims, preferred_element_type=F32)


def kernel(
    q_hbm, do_hbm, kt_hbm, gain_ref, groups_ref,
    gq_hbm, gk_ref, gg_ref,
    qp, do_raw, do_f32, dop, kt, kr, st, dpt, ds, pw,
    stat, stat_in, h1, h2, h1_in, h2_in, t1, h1b, h1b_in, t2, t2_in,
    ga, ga_in, gb, gb_in, gc, gc_in, dq, dq_in, gq,
    local_sem, send_sem, recv_sem,
):
    x = lax.axis_index("dp")
    ctx = lax.axis_index("ctx")
    exp = lax.axis_index("exp")
    zh, core = ctx // CORES, ctx % CORES
    y, zl = exp // ZL, exp % ZL

    def device(dx=0, dy=0, dz=0, dc=0):
        z = (zh * ZL + zl + dz) % (ZH * ZL)
        return (
            (x + dx) % X,
            (z // ZL) * CORES + (core + dc) % CORES,
            ((y + dy) % Y) * ZL + z % ZL,
        )

    count = [0]

    def remote(src, dst, **where):
        i = count[0]
        count[0] += 1
        return pltpu.make_async_remote_copy(
            src_ref=src, dst_ref=dst, send_sem=send_sem.at[i], recv_sem=recv_sem.at[i],
            device_id=device(**where), device_id_type=MESH_ID,
        )

    loads = [pltpu.make_async_copy(kt_hbm, kt.at[0], local_sem.at[0])]
    loads.append(pltpu.make_async_copy(do_hbm, do_raw, local_sem.at[1]))
    for h in range(4):
        loads.append(
            pltpu.make_async_copy(
                q_hbm.at[h], qp.at[h // 2, :, pl.ds((h % 2) * 128, 128)], local_sem.at[2 + h]
            )
        )
    for copy in loads:
        copy.start()

    barrier = pltpu.get_barrier_semaphore()
    peers = [dict(dz=d) for d in Z_PEERS]
    peers += [dict(dy=d) for d in Y_PEERS]
    peers += [dict(dx=d, dc=c) for d, c in X_PEERS]
    for peer in peers:
        pl.semaphore_signal(barrier, inc=1, device_id=device(**peer), device_id_type=MESH_ID)
    loads[0].wait()
    pl.semaphore_wait(barrier, len(peers))

    p0 = (y % 4) * QUARTER
    first = {}
    for rel in (1, 2):
        for at, (off, rows) in enumerate(PIECES):
            part = pl.ds(pl.multiple_of(p0 + off, 16), rows)
            first[rel, at] = remote(kt.at[0, part], kt.at[rel, part], dz=(ZH - rel) * ZL)
            first[rel, at].start()

    for copy in loads[2:]:
        copy.wait()
    swap_q = remote(qp.at[pl.ds(0, 2)], qp.at[pl.ds(2, 2)], dc=1)
    swap_q.start()
    loads[1].wait()
    do_f32[...] = do_raw[...].astype(F32)
    for h in range(4):
        dop[h // 2, pl.ds((h % 2) * 128, 128), :] = do_f32[:, h, :].astype(BF16)
    swap_do = remote(dop.at[pl.ds(0, 2)], dop.at[pl.ds(2, 2)], dc=1)
    swap_do.start()

    second = {1: [], 2: []}
    for rel in (1, 2):
        for at, (off, rows) in enumerate(PIECES):
            first[rel, at].wait_recv()
            part = pl.ds(pl.multiple_of(p0 + off, 16), rows)
            for dy in (1, Y - 1, 2 if at == 0 else Y - 2):
                copy = remote(kt.at[rel, part], kt.at[rel, part], dy=dy)
                copy.start()
                second[rel].append(copy)

    swap_q.wait_recv()
    swap_do.wait_recv()

    def keys_in(rel):
        for c in range(0, LATENT, 128):
            kr[rel, :, c : c + 128] = kt[rel, c : c + 128, :].astype(F32).T.astype(BF16)
        kr[rel, :, LATENT:] = kt[rel, LATENT:, :].astype(F32).T.astype(BF16)

    diff = lax.broadcasted_iota(jnp.int32, (128, 256), 0) - (
        lax.broadcasted_iota(jnp.int32, (128, 256), 1) & 127
    )
    group = (groups_ref[0, ctx], groups_ref[0, zh * CORES + 1 - core])

    def score(rel):
        base = ((zh + rel) % ZH) * CORES + core
        keys = kr[rel]
        for cc in range(4):
            visible = diff <= (group[cc // 2] - base) * 128
            s = dot(keys, qp[cc]) * SCALE
            st[cc, pl.ds(rel * 128, 128), :] = jnp.where(visible, s, MASKED)
            dpt[cc, pl.ds(rel * 128, 128), :] = dot(keys[:, :LATENT], dop[cc], NT)

    keys_in(0)
    score(0)
    for rel in (1, 2):
        for copy in second[rel]:
            copy.wait_recv()
        keys_in(rel)
        score(rel)

    for cc in range(4):
        s = st[cc]
        m = jnp.max(s, axis=0, keepdims=True)
        p = jnp.where(s > 0.5 * MASKED, jnp.exp(s - m), 0.0)
        st[cc] = p
        stat[cc, 0:1, :] = m
        stat[cc, 1:2, :] = jnp.sum(p, axis=0, keepdims=True)
        stat[cc, 2:3, :] = jnp.sum(p * dpt[cc], axis=0, keepdims=True)
        stat[cc, 3:8, :] = jnp.zeros((5, 256), F32)
    swap_stat = remote(stat, stat_in, dc=1)
    swap_stat.start()
    swap_stat.wait_recv()

    for cc in range(4):
        other = (cc + 2) % 4
        m0, l0, w0 = stat[cc, 0:1, :], stat[cc, 1:2, :], stat[cc, 2:3, :]
        m1, l1, w1 = stat_in[other, 0:1, :], stat_in[other, 1:2, :], stat_in[other, 2:3, :]
        m = jnp.maximum(m0, m1)
        e0, e1 = jnp.exp(m0 - m), jnp.exp(m1 - m)
        inv = 1.0 / (l0 * e0 + l1 * e1)
        delta = (w0 * e0 + w1 * e1) * inv
        w = st[cc] * (e0 * inv)
        pw[cc] = w.astype(BF16)
        ds[cc] = (w * (dpt[cc] - delta)).astype(BF16)

    def picks(rows, wanted):
        out_row = lax.broadcasted_iota(jnp.int32, (rows, 128), 0)
        in_row = lax.broadcasted_iota(jnp.int32, (rows, 128), 1)
        return (in_row == wanted(out_row)).astype(BF16)

    by_z = picks(128, lambda o: ((o & 31) >> 2) * 16 + (o >> 5) * 4 + (o & 3))
    by_z_low = picks(64, lambda o: ((o & 15) >> 2) * 16 + (o >> 4) * 4 + (o & 3))
    by_z_high = picks(64, lambda o: (((o & 15) >> 2) + 4) * 16 + (o >> 4) * 4 + (o & 3))
    gain = jnp.zeros((1, LATENT), F32)

    def key_part(rel, gain):
        rows = pl.ds(rel * 128, 128)
        dk = dot(ds[0, rows, :], qp[0], NT)
        dv = dot(pw[0, rows, :], dop[0])
        for cc in range(1, 4):
            dk = dk + dot(ds[cc, rows, :], qp[cc], NT)
            dv = dv + dot(pw[cc, rows, :], dop[cc])
        dk = dk * SCALE
        full = dk[:, :LATENT] + dv
        h1[rel] = full[:, :COLS_Y].astype(BF16)
        main = dot(by_z, full[:, COLS_Y:].astype(BF16)).astype(BF16)
        rope = dk[:, LATENT:].astype(BF16)
        low = dot(by_z_low, rope)
        high = dot(by_z_high, rope)
        side = jnp.concatenate([low, high], axis=1).astype(BF16)
        for l in range(ZL):
            h2[rel, l, 0:32, :] = main[l * 32 : l * 32 + 32, :]
            h2[rel, l, 32:48, :] = side[l * 16 : l * 16 + 16, :]
        return gain + jnp.sum(full * kr[rel, :, :LATENT].astype(F32), axis=0, keepdims=True)

    def pack(row, ref):
        for t in range(4):
            ref[t : t + 1, :] = row[:, t * 128 : (t + 1) * 128]
        ref[4:8, :] = jnp.zeros((4, 128), F32)

    def y_rows(dy):
        return pl.ds(pl.multiple_of(((y + dy) % Y) * 16, 16), 16)

    def z_at(dz):
        z = (zh * ZL + zl + dz) % (ZH * ZL)
        return (z // ZL + ZH - zh) % ZH, z % ZL

    for rel in (1, 2):
        gain = key_part(rel, gain)
    stage_z = [remote(h2.at[z_at(d)], h2_in.at[i], dz=d) for i, d in enumerate(Z_PEERS)]
    for copy in stage_z[:Z_FAR]:
        copy.start()
    gain = key_part(0, gain)
    stage_y = [remote(h1.at[:, y_rows(d), :], h1_in.at[i], dy=d) for i, d in enumerate(Y_PEERS)]
    for copy in stage_y[:3]:
        copy.start()
    pack(gain, ga)
    gain_a = [remote(ga, ga_in.at[i], dx=d, dc=c) for i, (d, c) in enumerate(X_PEERS)]
    for copy in gain_a:
        copy.start()
    for copy in stage_z[Z_FAR:] + stage_y[3:]:
        copy.start()

    def query_part(cc):
        total = dot(kt[0], ds[cc, 0:128, :])
        for rel in (1, 2):
            total = total + dot(kt[rel], ds[cc, rel * 128 : rel * 128 + 128, :])
        return total * SCALE

    swap_dq = []
    for cc in (2, 3):
        dq[cc - 2] = query_part(cc)
        copy = remote(dq.at[cc - 2], dq_in.at[cc - 2], dc=1)
        copy.start()
        swap_dq.append(copy)

    for copy in gain_a:
        copy.wait_recv()
    total = ga[...]
    for i in range(len(X_PEERS)):
        total = total + ga_in[i]
    gb[...] = total
    gain_b = [remote(gb, gb_in.at[i], dy=d) for i, d in enumerate(Y_PEERS)]
    for copy in gain_b:
        copy.start()

    stores = []
    for cc in range(2):
        own = query_part(cc)
        swap_dq[cc].wait_recv()
        gq[cc] = (own + dq_in[cc]).astype(BF16)
        for h in range(2):
            store = pltpu.make_async_copy(
                gq.at[cc, :, pl.ds(h * 128, 128)], gq_hbm.at[cc * 2 + h],
                local_sem.at[6 + cc * 2 + h],
            )
            store.start()
            stores.append(store)

    t1[...] = jnp.zeros_like(t1)
    for copy in stage_y:
        copy.wait_recv()
    for rel in range(3):
        part = h1[rel, y_rows(0), :].astype(F32)
        for i in range(len(Y_PEERS)):
            part = part + h1_in[i, rel].astype(F32)
        for l in range(ZL):
            for t in range(3):
                t1[rel, l, t * 4 : t * 4 + 4, :] = part[l * 4 : l * 4 + 4, t * 128 : (t + 1) * 128]
    h1b[...] = t1[...].astype(BF16)
    stage_yz = [
        remote(h1b.at[z_at(d)], h1b_in.at[i], dz=d) for i, d in enumerate(Z_PEERS)
    ]
    for copy in stage_yz:
        copy.start()

    for copy in stage_z:
        copy.wait_recv()
    part = h2[0, zl].astype(F32)
    for i in range(len(Z_PEERS)):
        part = part + h2_in[i].astype(F32)
    for yy in range(Y):
        t2[yy, 0:4, :] = part[yy * 4 : yy * 4 + 4, :]
        t2[yy, 4:8, :] = part[32 + (yy % 4) * 4 : 36 + (yy % 4) * 4, :]
    stage_zy = [remote(t2.at[(y + d) % Y], t2_in.at[i], dy=d) for i, d in enumerate(Y_PEERS)]
    for copy in stage_zy:
        copy.start()

    for copy in gain_b:
        copy.wait_recv()
    total = gb[...]
    for i in range(len(Y_PEERS)):
        total = total + gb_in[i]
    gc[...] = total
    gain_c = [remote(gc, gc_in.at[i], dz=d) for i, d in enumerate(Z_PEERS)]
    for copy in gain_c:
        copy.start()

    for copy in stage_yz:
        copy.wait_recv()
    part = t1[0, zl]
    for i in range(len(Z_PEERS)):
        part = part + h1b_in[i].astype(F32)
    for t in range(3):
        gk_ref[:, t * 128 : (t + 1) * 128] = part[t * 4 : t * 4 + 4, :]
    for copy in stage_zy:
        copy.wait_recv()
    part = t2[y]
    for i in range(len(Y_PEERS)):
        part = part + t2_in[i]
    gk_ref[:, COLS_Y:LATENT] = part[0:4, :]
    gk_ref[:, LATENT:] = jnp.where(y < Y // 2, part[4:8, :ROPE], part[4:8, ROPE:])
    for copy in gain_c:
        copy.wait_recv()
    total = gc[...]
    for i in range(len(Z_PEERS)):
        total = total + gc_in[i]
    gg_ref[...] = total[0:4, :] / gain_ref[...]

    for copy in stores:
        copy.wait()
    sent = list(first.values()) + second[1] + second[2] + [swap_q, swap_do, swap_stat] + swap_dq
    sent += gain_a + gain_b + gain_c + stage_y + stage_z + stage_yz + stage_zy
    for copy in sent:
        copy.wait_send()


N_COPIES = 4 + 12 + 3 + 2 + len(X_PEERS) + 3 * len(Y_PEERS) + 3 * len(Z_PEERS)


def finish(gq_in, gk_in, gg_in, gq_out, gk_out, gg_out, sem):
    copies = [
        pltpu.make_async_copy(gq_in, gq_out, sem.at[0]),
        pltpu.make_async_copy(gk_in, gk_out, sem.at[1]),
        pltpu.make_async_copy(gg_in, gg_out, sem.at[2]),
    ]
    for copy in copies:
        copy.start()
    for copy in copies:
        copy.wait()


def body(queries, out_grad, latent_keys, kv_gain, query_groups):
    q_t = jnp.transpose(queries[0], (1, 2, 0))
    k_t = jnp.transpose(latent_keys[0], (1, 0))
    any_spec = pl.BlockSpec(memory_space=pl.ANY)
    hbm_spec = pl.BlockSpec(memory_space=pltpu.HBM)
    vmem_spec = pl.BlockSpec(memory_space=pltpu.VMEM)
    ny, nz, nx = len(Y_PEERS), len(Z_PEERS), len(X_PEERS)
    results = (
        jax.ShapeDtypeStruct((4, WIDTH, 128), BF16),
        jax.ShapeDtypeStruct((4, WIDTH), F32),
        jax.ShapeDtypeStruct((4, 128), F32),
    )
    gq, gk, gg = pl.pallas_call(
        kernel,
        out_shape=results,
        in_specs=[hbm_spec, hbm_spec, hbm_spec, vmem_spec, pl.BlockSpec(memory_space=pltpu.SMEM)],
        out_specs=(any_spec, vmem_spec, vmem_spec),
        scratch_shapes=[
            pltpu.VMEM((4, WIDTH, 256), BF16),
            pltpu.VMEM((128, 4, LATENT), BF16),
            pltpu.VMEM((128, 4, LATENT), F32),
            pltpu.VMEM((4, 256, LATENT), BF16),
            pltpu.VMEM((3, WIDTH, 128), BF16),
            pltpu.VMEM((3, 128, WIDTH), BF16),
            pltpu.VMEM((4, 384, 256), F32),
            pltpu.VMEM((4, 384, 256), F32),
            pltpu.VMEM((4, 384, 256), BF16),
            pltpu.VMEM((4, 384, 256), BF16),
            pltpu.VMEM((4, 8, 256), F32),
            pltpu.VMEM((4, 8, 256), F32),
            pltpu.VMEM((3, 128, COLS_Y), BF16),
            pltpu.VMEM((3, ZL, 48, 128), BF16),
            pltpu.VMEM((ny, 3, 16, COLS_Y), BF16),
            pltpu.VMEM((nz, 48, 128), BF16),
            pltpu.VMEM((3, ZL, 16, 128), F32),
            pltpu.VMEM((3, ZL, 16, 128), BF16),
            pltpu.VMEM((nz, 16, 128), BF16),
            pltpu.VMEM((Y, 8, 128), F32),
            pltpu.VMEM((ny, 8, 128), F32),
            pltpu.VMEM((8, 128), F32),
            pltpu.VMEM((nx, 8, 128), F32),
            pltpu.VMEM((8, 128), F32),
            pltpu.VMEM((ny, 8, 128), F32),
            pltpu.VMEM((8, 128), F32),
            pltpu.VMEM((nz, 8, 128), F32),
            pltpu.VMEM((2, WIDTH, 256), F32),
            pltpu.VMEM((2, WIDTH, 256), F32),
            pltpu.VMEM((2, WIDTH, 256), BF16),
            pltpu.SemaphoreType.DMA((10,)),
            pltpu.SemaphoreType.DMA((N_COPIES,)),
            pltpu.SemaphoreType.DMA((N_COPIES,)),
        ],
        compiler_params=pltpu.CompilerParams(
            collective_id=0, has_side_effects=True, vmem_limit_bytes=60 * 2**20
        ),
        cost_estimate=pl.CostEstimate(
            flops=5 * 2 * 512 * 768 * 550, bytes_accessed=3 * 2**20, transcendentals=512 * 768
        ),
        name="mla_backward",
    )(q_t, out_grad[0], k_t, kv_gain.reshape(4, 128), query_groups)
    gq, gk, gg = pl.pallas_call(
        finish,
        out_shape=results,
        in_specs=[any_spec] * 3,
        out_specs=(any_spec,) * 3,
        scratch_shapes=[pltpu.SemaphoreType.DMA((3,))],
        compiler_params=pltpu.CompilerParams(vmem_limit_bytes=60 * 2**20),
        name="results",
    )(gq, gk, gg)
    grad_queries = jnp.transpose(gq, (2, 0, 1))[None]
    return grad_queries, gk.reshape(1, 1, 4, WIDTH), gg.reshape(LATENT)


def solution(mesh):
    in_specs = (
        P("dp", "ctx", "exp", None),
        P("dp", "ctx", "exp", None),
        P("dp", "ctx", None),
        P(),
        P("dp", None),
    )
    out_specs = (P("dp", "ctx", "exp", None), P("dp", "ctx", "exp", None), P())
    return jax.shard_map(body, mesh=mesh, in_specs=in_specs, out_specs=out_specs, check_vma=False)
```

```python
import math

import jax
import jax.numpy as jnp
from jax import lax
from jax.experimental import pallas as pl
from jax.experimental.pallas import tpu as pltpu
from jax.sharding import PartitionSpec as P

LATENT = 512
WIDTH = 576
ROPE = WIDTH - LATENT
SCALE = (0.1 * math.log(40.0) + 1.0) ** 2 / math.sqrt(192.0)
MASKED = -1e30
MESH_ID = pl.DeviceIdType.MESH
F32 = jnp.float32
BF16 = jnp.bfloat16

X, Y, ZH, ZL, CORES = 4, 8, 3, 4, 2
QUARTER = WIDTH // 4
PIECES = ((0, 80), (80, 64))
Y_PEERS = (4, 3, 5, 2, 6, 1, 7)
Z_PEERS = (6, 5, 7, 4, 8, 3, 9, 2, 10, 1, 11)
Z_FAR = 5
X_PEERS = ((0, 1), (1, 0), (3, 0), (2, 0), (1, 1), (3, 1), (2, 1))
COLS_Y = 384
NT = (((1,), (1,)), ((), ()))
NN = (((1,), (0,)), ((), ()))


def dot(a, b, dims=NN):
    return lax.dot_general(a, b, dims, preferred_element_type=F32)


def kernel(
    q_hbm, do_hbm, kt_hbm, gain_ref, groups_ref,
    gq_hbm, gk_ref, gg_ref,
    qp, do_raw, do_f32, dop, kt, kr, st, dpt, ds, pw,
    stat, stat_in, h1, h2, h1_in, h2_in, t1, h1b, h1b_in, t2, t2_in,
    ga, ga_in, gb, gb_in, gc, gc_in, dq, dq_in, dq_own, gq,
    local_sem, send_sem, recv_sem,
):
    x = lax.axis_index("dp")
    ctx = lax.axis_index("ctx")
    exp = lax.axis_index("exp")
    zh, core = ctx // CORES, ctx % CORES
    y, zl = exp // ZL, exp % ZL

    def device(dx=0, dy=0, dz=0, dc=0):
        z = (zh * ZL + zl + dz) % (ZH * ZL)
        return (
            (x + dx) % X,
            (z // ZL) * CORES + (core + dc) % CORES,
            ((y + dy) % Y) * ZL + z % ZL,
        )

    count = [0]

    def remote(src, dst, **where):
        i = count[0]
        count[0] += 1
        return pltpu.make_async_remote_copy(
            src_ref=src, dst_ref=dst, send_sem=send_sem.at[i], recv_sem=recv_sem.at[i],
            device_id=device(**where), device_id_type=MESH_ID,
        )

    loads = [pltpu.make_async_copy(kt_hbm, kt.at[0], local_sem.at[0])]
    loads.append(pltpu.make_async_copy(do_hbm, do_raw, local_sem.at[1]))
    for h in range(4):
        loads.append(
            pltpu.make_async_copy(
                q_hbm.at[h], qp.at[h // 2, :, pl.ds((h % 2) * 128, 128)], local_sem.at[2 + h]
            )
        )
    for copy in loads:
        copy.start()

    barrier = pltpu.get_barrier_semaphore()
    peers = [dict(dz=d) for d in (4, 8, 2, 10, 1, 11)]
    peers += [dict(dy=d) for d in (2, 6, 1, 7)]
    peers += [dict(dx=d) for d in (2, 1, 3)] + [dict(dc=1)]
    for peer in peers:
        pl.semaphore_signal(barrier, inc=1, device_id=device(**peer), device_id_type=MESH_ID)
    loads[0].wait()
    pl.semaphore_wait(barrier, len(peers))

    p0 = (y % 4) * QUARTER
    first = {}
    for rel in (1, 2):
        for at, (off, rows) in enumerate(PIECES):
            part = pl.ds(pl.multiple_of(p0 + off, 16), rows)
            first[rel, at] = remote(kt.at[0, part], kt.at[rel, part], dz=(ZH - rel) * ZL)
            first[rel, at].start()

    for copy in loads[2:]:
        copy.wait()
    swap_q = remote(qp.at[pl.ds(0, 2)], qp.at[pl.ds(2, 2)], dc=1)
    swap_q.start()
    loads[1].wait()
    do_f32[...] = do_raw[...].astype(F32)
    for h in range(4):
        dop[h // 2, pl.ds((h % 2) * 128, 128), :] = do_f32[:, h, :].astype(BF16)
    swap_do = remote(dop.at[pl.ds(0, 2)], dop.at[pl.ds(2, 2)], dc=1)
    swap_do.start()

    second = {1: [], 2: []}
    for rel in (1, 2):
        for at, (off, rows) in enumerate(PIECES):
            first[rel, at].wait_recv()
            part = pl.ds(pl.multiple_of(p0 + off, 16), rows)
            for dy in (1, Y - 1, 2 if at == 0 else Y - 2):
                copy = remote(kt.at[rel, part], kt.at[rel, part], dy=dy)
                copy.start()
                second[rel].append(copy)

    swap_q.wait_recv()
    swap_do.wait_recv()

    def keys_in(rel):
        for c in range(0, LATENT, 128):
            kr[rel, :, c : c + 128] = kt[rel, c : c + 128, :].astype(F32).T.astype(BF16)
        kr[rel, :, LATENT:] = kt[rel, LATENT:, :].astype(F32).T.astype(BF16)

    diff = lax.broadcasted_iota(jnp.int32, (128, 256), 0) - (
        lax.broadcasted_iota(jnp.int32, (128, 256), 1) & 127
    )
    group = (groups_ref[0, ctx], groups_ref[0, zh * CORES + 1 - core])

    def score(rel):
        base = ((zh + rel) % ZH) * CORES + core
        keys = kr[rel]
        for cc in range(4):
            visible = diff <= (group[cc // 2] - base) * 128
            s = dot(keys, qp[cc]) * SCALE
            st[cc, pl.ds(rel * 128, 128), :] = jnp.where(visible, s, MASKED)
            dpt[cc, pl.ds(rel * 128, 128), :] = dot(keys[:, :LATENT], dop[cc], NT)

    keys_in(0)
    score(0)
    for rel in (1, 2):
        for copy in second[rel]:
            copy.wait_recv()
        keys_in(rel)
        score(rel)

    for cc in range(4):
        s = st[cc]
        m = jnp.max(s, axis=0, keepdims=True)
        p = jnp.where(s > 0.5 * MASKED, jnp.exp(s - m), 0.0)
        st[cc] = p
        stat[cc, 0:1, :] = m
        stat[cc, 1:2, :] = jnp.sum(p, axis=0, keepdims=True)
        stat[cc, 2:3, :] = jnp.sum(p * dpt[cc], axis=0, keepdims=True)
        stat[cc, 3:8, :] = jnp.zeros((5, 256), F32)
    swap_stat = remote(stat, stat_in, dc=1)
    swap_stat.start()
    swap_stat.wait_recv()

    for cc in range(4):
        other = (cc + 2) % 4
        m0, l0, w0 = stat[cc, 0:1, :], stat[cc, 1:2, :], stat[cc, 2:3, :]
        m1, l1, w1 = stat_in[other, 0:1, :], stat_in[other, 1:2, :], stat_in[other, 2:3, :]
        m = jnp.maximum(m0, m1)
        e0, e1 = jnp.exp(m0 - m), jnp.exp(m1 - m)
        inv = 1.0 / (l0 * e0 + l1 * e1)
        delta = (w0 * e0 + w1 * e1) * inv
        w = st[cc] * (e0 * inv)
        pw[cc] = w.astype(BF16)
        ds[cc] = (w * (dpt[cc] - delta)).astype(BF16)

    def picks(rows, wanted):
        out_row = lax.broadcasted_iota(jnp.int32, (rows, 128), 0)
        in_row = lax.broadcasted_iota(jnp.int32, (rows, 128), 1)
        return (in_row == wanted(out_row)).astype(BF16)

    by_z = picks(128, lambda o: ((o & 31) >> 2) * 16 + (o >> 5) * 4 + (o & 3))
    by_z_low = picks(64, lambda o: ((o & 15) >> 2) * 16 + (o >> 4) * 4 + (o & 3))
    by_z_high = picks(64, lambda o: (((o & 15) >> 2) + 4) * 16 + (o >> 4) * 4 + (o & 3))
    gain = jnp.zeros((1, LATENT), F32)

    def key_part(rel, gain):
        rows = pl.ds(rel * 128, 128)
        dk = dot(ds[0, rows, :], qp[0], NT)
        dv = dot(pw[0, rows, :], dop[0])
        for cc in range(1, 4):
            dk = dk + dot(ds[cc, rows, :], qp[cc], NT)
            dv = dv + dot(pw[cc, rows, :], dop[cc])
        dk = dk * SCALE
        full = dk[:, :LATENT] + dv
        h1[rel] = full[:, :COLS_Y].astype(BF16)
        main = dot(by_z, full[:, COLS_Y:].astype(BF16)).astype(BF16)
        rope = dk[:, LATENT:].astype(BF16)
        low = dot(by_z_low, rope)
        high = dot(by_z_high, rope)
        side = jnp.concatenate([low, high], axis=1).astype(BF16)
        for l in range(ZL):
            h2[rel, l, 0:32, :] = main[l * 32 : l * 32 + 32, :]
            h2[rel, l, 32:48, :] = side[l * 16 : l * 16 + 16, :]
        return gain + jnp.sum(full * kr[rel, :, :LATENT].astype(F32), axis=0, keepdims=True)

    def pack(row, ref):
        for t in range(4):
            ref[t : t + 1, :] = row[:, t * 128 : (t + 1) * 128]
        ref[4:8, :] = jnp.zeros((4, 128), F32)

    def y_rows(dy):
        return pl.ds(pl.multiple_of(((y + dy) % Y) * 16, 16), 16)

    def z_at(dz):
        z = (zh * ZL + zl + dz) % (ZH * ZL)
        return (z // ZL + ZH - zh) % ZH, z % ZL

    for rel in (1, 2):
        gain = key_part(rel, gain)
    stage_z = [remote(h2.at[z_at(d)], h2_in.at[i], dz=d) for i, d in enumerate(Z_PEERS)]
    for copy in stage_z[:Z_FAR]:
        copy.start()
    gain = key_part(0, gain)
    stage_y = [remote(h1.at[:, y_rows(d), :], h1_in.at[i], dy=d) for i, d in enumerate(Y_PEERS)]
    for copy in stage_y[:3]:
        copy.start()
    pack(gain, ga)
    gain_a = [remote(ga, ga_in.at[i], dx=d, dc=c) for i, (d, c) in enumerate(X_PEERS)]
    for copy in gain_a:
        copy.start()
    for copy in stage_z[Z_FAR:] + stage_y[3:]:
        copy.start()

    def query_part(cc):
        total = dot(kt[0], ds[cc, 0:128, :])
        for rel in (1, 2):
            total = total + dot(kt[rel], ds[cc, rel * 128 : rel * 128 + 128, :])
        return total * SCALE

    swap_dq = []
    for cc in (2, 3):
        dq[cc - 2] = query_part(cc)
        copy = remote(dq.at[cc - 2], dq_in.at[cc - 2], dc=1)
        copy.start()
        swap_dq.append(copy)

    for copy in gain_a:
        copy.wait_recv()
    total = ga[...]
    for i in range(len(X_PEERS)):
        total = total + ga_in[i]
    gb[...] = total
    gain_b = [remote(gb, gb_in.at[i], dy=d) for i, d in enumerate(Y_PEERS)]
    for copy in gain_b:
        copy.start()

    for cc in range(2):
        dq_own[cc] = query_part(cc)

    t1[...] = jnp.zeros_like(t1)
    for copy in stage_y:
        copy.wait_recv()
    for rel in range(3):
        part = h1[rel, y_rows(0), :].astype(F32)
        for i in range(len(Y_PEERS)):
            part = part + h1_in[i, rel].astype(F32)
        for l in range(ZL):
            for t in range(3):
                t1[rel, l, t * 4 : t * 4 + 4, :] = part[l * 4 : l * 4 + 4, t * 128 : (t + 1) * 128]
    h1b[...] = t1[...].astype(BF16)
    stage_yz = [
        remote(h1b.at[z_at(d)], h1b_in.at[i], dz=d) for i, d in enumerate(Z_PEERS)
    ]
    for copy in stage_yz:
        copy.start()

    for copy in gain_b:
        copy.wait_recv()
    total = gb[...]
    for i in range(len(Y_PEERS)):
        total = total + gb_in[i]
    gc[...] = total
    gain_c = [remote(gc, gc_in.at[i], dz=d) for i, d in enumerate(Z_PEERS)]
    for copy in gain_c:
        copy.start()

    for copy in stage_z:
        copy.wait_recv()
    part = h2[0, zl].astype(F32)
    for i in range(len(Z_PEERS)):
        part = part + h2_in[i].astype(F32)
    for yy in range(Y):
        t2[yy, 0:4, :] = part[yy * 4 : yy * 4 + 4, :]
        t2[yy, 4:8, :] = part[32 + (yy % 4) * 4 : 36 + (yy % 4) * 4, :]
    stage_zy = [remote(t2.at[(y + d) % Y], t2_in.at[i], dy=d) for i, d in enumerate(Y_PEERS)]
    for copy in stage_zy:
        copy.start()

    stores = []
    for cc in range(2):
        swap_dq[cc].wait_recv()
        gq[cc] = (dq_own[cc] + dq_in[cc]).astype(BF16)
        for h in range(2):
            store = pltpu.make_async_copy(
                gq.at[cc, :, pl.ds(h * 128, 128)], gq_hbm.at[cc * 2 + h],
                local_sem.at[6 + cc * 2 + h],
            )
            store.start()
            stores.append(store)

    for copy in stage_yz:
        copy.wait_recv()
    part = t1[0, zl]
    for i in range(len(Z_PEERS)):
        part = part + h1b_in[i].astype(F32)
    for t in range(3):
        gk_ref[:, t * 128 : (t + 1) * 128] = part[t * 4 : t * 4 + 4, :]
    for copy in stage_zy:
        copy.wait_recv()
    part = t2[y]
    for i in range(len(Y_PEERS)):
        part = part + t2_in[i]
    gk_ref[:, COLS_Y:LATENT] = part[0:4, :]
    gk_ref[:, LATENT:] = jnp.where(y < Y // 2, part[4:8, :ROPE], part[4:8, ROPE:])
    for copy in gain_c:
        copy.wait_recv()
    total = gc[...]
    for i in range(len(Z_PEERS)):
        total = total + gc_in[i]
    gg_ref[...] = total[0:4, :] / gain_ref[...]

    for copy in stores:
        copy.wait()
    sent = list(first.values()) + second[1] + second[2] + [swap_q, swap_do, swap_stat] + swap_dq
    sent += gain_a + gain_b + gain_c + stage_y + stage_z + stage_yz + stage_zy
    for copy in sent:
        copy.wait_send()


N_COPIES = 4 + 12 + 3 + 2 + len(X_PEERS) + 3 * len(Y_PEERS) + 3 * len(Z_PEERS)


def finish(gq_in, gk_in, gg_in, gq_out, gk_out, gg_out, gq, gk, gg, in_sem, out_sem):
    views = [(gq_in.at[h], gq.at[h], gq_out.at[h]) for h in range(4)]
    views += [(gk_in, gk, gk_out), (gg_in, gg, gg_out)]
    loads = [pltpu.make_async_copy(a, b, in_sem.at[i]) for i, (a, b, _) in enumerate(views)]
    stores = [pltpu.make_async_copy(b, c, out_sem.at[i]) for i, (_, b, c) in enumerate(views)]
    for copy in loads:
        copy.start()
    for load, store in zip(loads, stores):
        load.wait()
        store.start()
    for copy in stores:
        copy.wait()


def body(queries, out_grad, latent_keys, kv_gain, query_groups):
    q_t = jnp.transpose(queries[0], (1, 2, 0))
    k_t = jnp.transpose(latent_keys[0], (1, 0))
    any_spec = pl.BlockSpec(memory_space=pl.ANY)
    hbm_spec = pl.BlockSpec(memory_space=pltpu.HBM)
    vmem_spec = pl.BlockSpec(memory_space=pltpu.VMEM)
    ny, nz, nx = len(Y_PEERS), len(Z_PEERS), len(X_PEERS)
    results = (
        jax.ShapeDtypeStruct((4, WIDTH, 128), BF16),
        jax.ShapeDtypeStruct((4, WIDTH), F32),
        jax.ShapeDtypeStruct((4, 128), F32),
    )
    gq, gk, gg = pl.pallas_call(
        kernel,
        out_shape=results,
        in_specs=[hbm_spec, hbm_spec, hbm_spec, vmem_spec, pl.BlockSpec(memory_space=pltpu.SMEM)],
        out_specs=(any_spec, vmem_spec, vmem_spec),
        scratch_shapes=[
            pltpu.VMEM((4, WIDTH, 256), BF16),
            pltpu.VMEM((128, 4, LATENT), BF16),
            pltpu.VMEM((128, 4, LATENT), F32),
            pltpu.VMEM((4, 256, LATENT), BF16),
            pltpu.VMEM((3, WIDTH, 128), BF16),
            pltpu.VMEM((3, 128, WIDTH), BF16),
            pltpu.VMEM((4, 384, 256), F32),
            pltpu.VMEM((4, 384, 256), F32),
            pltpu.VMEM((4, 384, 256), BF16),
            pltpu.VMEM((4, 384, 256), BF16),
            pltpu.VMEM((4, 8, 256), F32),
            pltpu.VMEM((4, 8, 256), F32),
            pltpu.VMEM((3, 128, COLS_Y), BF16),
            pltpu.VMEM((3, ZL, 48, 128), BF16),
            pltpu.VMEM((ny, 3, 16, COLS_Y), BF16),
            pltpu.VMEM((nz, 48, 128), BF16),
            pltpu.VMEM((3, ZL, 16, 128), F32),
            pltpu.VMEM((3, ZL, 16, 128), BF16),
            pltpu.VMEM((nz, 16, 128), BF16),
            pltpu.VMEM((Y, 8, 128), F32),
            pltpu.VMEM((ny, 8, 128), F32),
            pltpu.VMEM((8, 128), F32),
            pltpu.VMEM((nx, 8, 128), F32),
            pltpu.VMEM((8, 128), F32),
            pltpu.VMEM((ny, 8, 128), F32),
            pltpu.VMEM((8, 128), F32),
            pltpu.VMEM((nz, 8, 128), F32),
            pltpu.VMEM((2, WIDTH, 256), F32),
            pltpu.VMEM((2, WIDTH, 256), F32),
            pltpu.VMEM((2, WIDTH, 256), F32),
            pltpu.VMEM((2, WIDTH, 256), BF16),
            pltpu.SemaphoreType.DMA((10,)),
            pltpu.SemaphoreType.DMA((N_COPIES,)),
            pltpu.SemaphoreType.DMA((N_COPIES,)),
        ],
        compiler_params=pltpu.CompilerParams(
            collective_id=0, has_side_effects=True, vmem_limit_bytes=60 * 2**20
        ),
        cost_estimate=pl.CostEstimate(
            flops=5 * 2 * 512 * 768 * 550, bytes_accessed=3 * 2**20, transcendentals=512 * 768
        ),
        name="mla_backward",
    )(q_t, out_grad[0], k_t, kv_gain.reshape(4, 128), query_groups)
    gq, gk, gg = pl.pallas_call(
        finish,
        out_shape=results,
        in_specs=[any_spec] * 3,
        out_specs=(any_spec,) * 3,
        scratch_shapes=[pltpu.VMEM(r.shape, r.dtype) for r in results]
        + [pltpu.SemaphoreType.DMA((6,)), pltpu.SemaphoreType.DMA((6,))],
        compiler_params=pltpu.CompilerParams(vmem_limit_bytes=60 * 2**20),
        name="results",
    )(gq, gk, gg)
    grad_queries = jnp.transpose(gq, (2, 0, 1))[None]
    return grad_queries, gk.reshape(1, 1, 4, WIDTH), gg.reshape(LATENT)


def solution(mesh):
    in_specs = (
        P("dp", "ctx", "exp", None),
        P("dp", "ctx", "exp", None),
        P("dp", "ctx", None),
        P(),
        P("dp", None),
    )
    out_specs = (P("dp", "ctx", "exp", None), P("dp", "ctx", "exp", None), P())
    return jax.shard_map(body, mesh=mesh, in_specs=in_specs, out_specs=out_specs, check_vma=False)
```

```python
import math

import jax
import jax.numpy as jnp
from jax import lax
from jax.experimental import pallas as pl
from jax.experimental.pallas import tpu as pltpu
from jax.sharding import PartitionSpec as P

LATENT = 512
WIDTH = 576
ROPE = WIDTH - LATENT
SCALE = (0.1 * math.log(40.0) + 1.0) ** 2 / math.sqrt(192.0)
MASKED = -1e30
MESH_ID = pl.DeviceIdType.MESH
F32 = jnp.float32
BF16 = jnp.bfloat16

X, Y, ZH, ZL, CORES = 4, 8, 3, 4, 2
QUARTER = WIDTH // 4
PIECES = ((0, 80), (80, 64))
Y_PEERS = (4, 3, 5, 2, 6, 1, 7)
Z_PEERS = (6, 5, 7, 4, 8, 3, 9, 2, 10, 1, 11)
Z_FAR = 5
X_PEERS = ((0, 1), (1, 0), (3, 0), (2, 0), (1, 1), (3, 1), (2, 1))
COLS_Y = 384
NT = (((1,), (1,)), ((), ()))
NN = (((1,), (0,)), ((), ()))


def dot(a, b, dims=NN):
    return lax.dot_general(a, b, dims, preferred_element_type=F32)


def kernel(
    q_hbm, do_hbm, kt_hbm, gain_hbm, groups_hbm,
    gq_ref, gk_ref, gg_ref,
    qp, do_raw, do_f32, dop, kt, kr, st, dpt, ds, pw,
    stat, stat_in, h1, h2, h1_in, h2_in, t1, h1b, h1b_in, t2, t2_in,
    ga, ga_in, gb, gb_in, gc, gc_in, dq, dq_in, dq_own, gain_ref, groups_ref,
    local_sem, send_sem, recv_sem,
):
    x = lax.axis_index("dp")
    ctx = lax.axis_index("ctx")
    exp = lax.axis_index("exp")
    zh, core = ctx // CORES, ctx % CORES
    y, zl = exp // ZL, exp % ZL

    def device(dx=0, dy=0, dz=0, dc=0):
        z = (zh * ZL + zl + dz) % (ZH * ZL)
        return (
            (x + dx) % X,
            (z // ZL) * CORES + (core + dc) % CORES,
            ((y + dy) % Y) * ZL + z % ZL,
        )

    count = [0]

    def remote(src, dst, **where):
        i = count[0]
        count[0] += 1
        return pltpu.make_async_remote_copy(
            src_ref=src, dst_ref=dst, send_sem=send_sem.at[i], recv_sem=recv_sem.at[i],
            device_id=device(**where), device_id_type=MESH_ID,
        )

    loads = [pltpu.make_async_copy(kt_hbm, kt.at[0], local_sem.at[0])]
    loads.append(pltpu.make_async_copy(do_hbm, do_raw, local_sem.at[1]))
    for h in range(4):
        loads.append(
            pltpu.make_async_copy(
                q_hbm.at[h], qp.at[h // 2, :, pl.ds((h % 2) * 128, 128)], local_sem.at[2 + h]
            )
        )
    tables = [
        pltpu.make_async_copy(gain_hbm, gain_ref, local_sem.at[6]),
        pltpu.make_async_copy(groups_hbm, groups_ref, local_sem.at[7]),
    ]
    loads[0].start()

    barrier = pltpu.get_barrier_semaphore()
    peers = [dict(dz=d) for d in (4, 8, 2, 10, 1, 11)]
    peers += [dict(dy=d) for d in (2, 6, 1, 7)]
    peers += [dict(dx=d) for d in (2, 1, 3)] + [dict(dc=1)]
    for peer in peers:
        pl.semaphore_signal(barrier, inc=1, device_id=device(**peer), device_id_type=MESH_ID)
    for copy in loads[1:] + tables:
        copy.start()
    loads[0].wait()
    pl.semaphore_wait(barrier, len(peers))

    p0 = (y % 4) * QUARTER
    first = {}
    for rel in (1, 2):
        for at, (off, rows) in enumerate(PIECES):
            part = pl.ds(pl.multiple_of(p0 + off, 16), rows)
            first[rel, at] = remote(kt.at[0, part], kt.at[rel, part], dz=(ZH - rel) * ZL)
            first[rel, at].start()

    for copy in loads[2:]:
        copy.wait()
    swap_q = remote(qp.at[pl.ds(0, 2)], qp.at[pl.ds(2, 2)], dc=1)
    swap_q.start()
    loads[1].wait()
    do_f32[...] = do_raw[...].astype(F32)
    for h in range(4):
        dop[h // 2, pl.ds((h % 2) * 128, 128), :] = do_f32[:, h, :].astype(BF16)
    swap_do = remote(dop.at[pl.ds(0, 2)], dop.at[pl.ds(2, 2)], dc=1)
    swap_do.start()

    second = {1: [], 2: []}
    for rel in (1, 2):
        for at, (off, rows) in enumerate(PIECES):
            first[rel, at].wait_recv()
            part = pl.ds(pl.multiple_of(p0 + off, 16), rows)
            for dy in (1, Y - 1, 2 if at == 0 else Y - 2):
                copy = remote(kt.at[rel, part], kt.at[rel, part], dy=dy)
                copy.start()
                second[rel].append(copy)

    swap_q.wait_recv()
    swap_do.wait_recv()
    for copy in tables:
        copy.wait()

    def keys_in(rel):
        for c in range(0, LATENT, 128):
            kr[rel, :, c : c + 128] = kt[rel, c : c + 128, :].astype(F32).T.astype(BF16)
        kr[rel, :, LATENT:] = kt[rel, LATENT:, :].astype(F32).T.astype(BF16)

    diff = lax.broadcasted_iota(jnp.int32, (128, 256), 0) - (
        lax.broadcasted_iota(jnp.int32, (128, 256), 1) & 127
    )
    group = (groups_ref[0, ctx], groups_ref[0, zh * CORES + 1 - core])

    parts = {}

    def score(rel):
        base = ((zh + rel) % ZH) * CORES + core
        rows = pl.ds(rel * 128, 128)
        keys = kr[rel]
        for cc in range(4):
            visible = diff <= (group[cc // 2] - base) * 128
            s = jnp.where(visible, dot(keys, qp[cc]) * SCALE, MASKED)
            dp = dot(keys[:, :LATENT], dop[cc], NT)
            m = jnp.max(s, axis=0, keepdims=True)
            p = jnp.where(visible, jnp.exp(s - m), 0.0)
            st[cc, rows, :] = p
            dpt[cc, rows, :] = dp
            parts[rel, cc] = (
                m, jnp.sum(p, axis=0, keepdims=True), jnp.sum(p * dp, axis=0, keepdims=True)
            )

    keys_in(0)
    score(0)
    for rel in (1, 2):
        for copy in second[rel]:
            copy.wait_recv()
        keys_in(rel)
        score(rel)

    for cc in range(4):
        m = jnp.maximum(jnp.maximum(parts[0, cc][0], parts[1, cc][0]), parts[2, cc][0])
        e = [jnp.exp(parts[rel, cc][0] - m) for rel in range(3)]
        stat[cc, 0:1, :] = m
        stat[cc, 1:2, :] = sum(parts[rel, cc][1] * e[rel] for rel in range(3))
        stat[cc, 2:3, :] = sum(parts[rel, cc][2] * e[rel] for rel in range(3))
        stat[cc, 3:8, :] = jnp.zeros((5, 256), F32)
    swap_stat = remote(stat, stat_in, dc=1)
    swap_stat.start()
    swap_stat.wait_recv()

    both = []
    for cc in range(4):
        other = (cc + 2) % 4
        m0, l0, w0 = stat[cc, 0:1, :], stat[cc, 1:2, :], stat[cc, 2:3, :]
        m1, l1, w1 = stat_in[other, 0:1, :], stat_in[other, 1:2, :], stat_in[other, 2:3, :]
        m = jnp.maximum(m0, m1)
        e0, e1 = jnp.exp(m0 - m), jnp.exp(m1 - m)
        inv = 1.0 / (l0 * e0 + l1 * e1)
        both.append((m, inv, (w0 * e0 + w1 * e1) * inv))

    def weigh(rel):
        rows = pl.ds(rel * 128, 128)
        for cc in range(4):
            m, inv, delta = both[cc]
            w = st[cc, rows, :] * (jnp.exp(parts[rel, cc][0] - m) * inv)
            pw[cc, rows, :] = w.astype(BF16)
            ds[cc, rows, :] = (w * (dpt[cc, rows, :] - delta)).astype(BF16)

    def picks(rows, wanted):
        out_row = lax.broadcasted_iota(jnp.int32, (rows, 128), 0)
        in_row = lax.broadcasted_iota(jnp.int32, (rows, 128), 1)
        return (in_row == wanted(out_row)).astype(BF16)

    by_z = picks(128, lambda o: ((o & 31) >> 2) * 16 + (o >> 5) * 4 + (o & 3))
    by_z_low = picks(64, lambda o: ((o & 15) >> 2) * 16 + (o >> 4) * 4 + (o & 3))
    by_z_high = picks(64, lambda o: (((o & 15) >> 2) + 4) * 16 + (o >> 4) * 4 + (o & 3))
    gain = jnp.zeros((1, LATENT), F32)

    def key_part(start, groups, gain):
        for rel in range(start, start + groups):
            weigh(rel)
        rows = pl.ds(start * 128, groups * 128)
        dk = dot(ds[0, rows, :], qp[0], NT)
        dv = dot(pw[0, rows, :], dop[0])
        for cc in range(1, 4):
            dk = dk + dot(ds[cc, rows, :], qp[cc], NT)
            dv = dv + dot(pw[cc, rows, :], dop[cc])
        dk = dk * SCALE
        dv = dk[:, :LATENT] + dv
        for g in range(groups):
            rel = start + g
            full = dv[g * 128 : g * 128 + 128]
            h1[rel] = full[:, :COLS_Y].astype(BF16)
            main = dot(by_z, full[:, COLS_Y:].astype(BF16)).astype(BF16)
            rope = dk[g * 128 : g * 128 + 128, LATENT:].astype(BF16)
            low = dot(by_z_low, rope)
            high = dot(by_z_high, rope)
            side = jnp.concatenate([low, high], axis=1).astype(BF16)
            for l in range(ZL):
                h2[rel, l, 0:32, :] = main[l * 32 : l * 32 + 32, :]
                h2[rel, l, 32:48, :] = side[l * 16 : l * 16 + 16, :]
            keys = kr[rel, :, :LATENT].astype(F32)
            gain = gain + jnp.sum(full * keys, axis=0, keepdims=True)
        return gain

    def pack(row, ref):
        for t in range(4):
            ref[t : t + 1, :] = row[:, t * 128 : (t + 1) * 128]
        ref[4:8, :] = jnp.zeros((4, 128), F32)

    def y_rows(dy):
        return pl.ds(pl.multiple_of(((y + dy) % Y) * 16, 16), 16)

    def z_at(dz):
        z = (zh * ZL + zl + dz) % (ZH * ZL)
        return (z // ZL + ZH - zh) % ZH, z % ZL

    gain = key_part(1, 2, gain)
    stage_z = [remote(h2.at[z_at(d)], h2_in.at[i], dz=d) for i, d in enumerate(Z_PEERS)]
    stage_y = [
        remote(h1.at[pl.ds(1, 2), y_rows(d), :], h1_in.at[i, pl.ds(1, 2)], dy=d)
        for i, d in enumerate(Y_PEERS)
    ]
    for i, copy in enumerate(stage_y):
        copy.start()
        if i < Z_FAR:
            stage_z[i].start()
    gain = key_part(0, 1, gain)
    last_y = [remote(h1.at[0, y_rows(d), :], h1_in.at[i, 0], dy=d) for i, d in enumerate(Y_PEERS)]
    pack(gain, ga)
    gain_a = [remote(ga, ga_in.at[i], dx=d, dc=c) for i, (d, c) in enumerate(X_PEERS)]
    for copy in last_y + gain_a + stage_z[Z_FAR:]:
        copy.start()
    stage_y = stage_y + last_y

    def query_part(cc):
        total = dot(kt[0], ds[cc, 0:128, :])
        for rel in (1, 2):
            total = total + dot(kt[rel], ds[cc, rel * 128 : rel * 128 + 128, :])
        return total * SCALE

    swap_dq = []
    for cc in (2, 3):
        dq[cc - 2] = query_part(cc)
        copy = remote(dq.at[cc - 2], dq_in.at[cc - 2], dc=1)
        copy.start()
        swap_dq.append(copy)

    for copy in gain_a:
        copy.wait_recv()
    total = ga[...]
    for i in range(len(X_PEERS)):
        total = total + ga_in[i]
    gb[...] = total
    gain_b = [remote(gb, gb_in.at[i], dy=d) for i, d in enumerate(Y_PEERS)]
    for copy in gain_b:
        copy.start()

    for cc in range(2):
        dq_own[cc] = query_part(cc)

    t1[...] = jnp.zeros_like(t1)
    for copy in stage_y:
        copy.wait_recv()
    for rel in range(3):
        part = h1[rel, y_rows(0), :].astype(F32)
        for i in range(len(Y_PEERS)):
            part = part + h1_in[i, rel].astype(F32)
        for l in range(ZL):
            for t in range(3):
                t1[rel, l, t * 4 : t * 4 + 4, :] = part[l * 4 : l * 4 + 4, t * 128 : (t + 1) * 128]
    h1b[...] = t1[...].astype(BF16)
    stage_yz = [
        remote(h1b.at[z_at(d)], h1b_in.at[i], dz=d) for i, d in enumerate(Z_PEERS)
    ]
    for copy in stage_yz:
        copy.start()

    for copy in gain_b:
        copy.wait_recv()
    total = gb[...]
    for i in range(len(Y_PEERS)):
        total = total + gb_in[i]
    gc[...] = total
    gain_c = [remote(gc, gc_in.at[i], dz=d) for i, d in enumerate(Z_PEERS)]
    for copy in gain_c:
        copy.start()

    for copy in stage_z:
        copy.wait_recv()
    part = h2[0, zl].astype(F32)
    for i in range(len(Z_PEERS)):
        part = part + h2_in[i].astype(F32)
    for yy in range(Y):
        t2[yy, 0:4, :] = part[yy * 4 : yy * 4 + 4, :]
        t2[yy, 4:8, :] = part[32 + (yy % 4) * 4 : 36 + (yy % 4) * 4, :]
    stage_zy = [remote(t2.at[(y + d) % Y], t2_in.at[i], dy=d) for i, d in enumerate(Y_PEERS)]
    for copy in stage_zy:
        copy.start()

    for cc in range(2):
        swap_dq[cc].wait_recv()
        full = (dq_own[cc] + dq_in[cc]).astype(BF16)
        gq_ref[cc * 2] = full[:, :128]
        gq_ref[cc * 2 + 1] = full[:, 128:]

    for copy in stage_yz:
        copy.wait_recv()
    part = t1[0, zl]
    for i in range(len(Z_PEERS)):
        part = part + h1b_in[i].astype(F32)
    for t in range(3):
        gk_ref[:, t * 128 : (t + 1) * 128] = part[t * 4 : t * 4 + 4, :]
    for copy in stage_zy:
        copy.wait_recv()
    part = t2[y]
    for i in range(len(Y_PEERS)):
        part = part + t2_in[i]
    gk_ref[:, COLS_Y:LATENT] = part[0:4, :]
    gk_ref[:, LATENT:] = jnp.where(y < Y // 2, part[4:8, :ROPE], part[4:8, ROPE:])
    for copy in gain_c:
        copy.wait_recv()
    total = gc[...]
    for i in range(len(Z_PEERS)):
        total = total + gc_in[i]
    gg_ref[...] = total[0:4, :] / gain_ref[...]

    sent = list(first.values()) + second[1] + second[2] + [swap_q, swap_do, swap_stat] + swap_dq
    sent += gain_a + gain_b + gain_c + stage_y + stage_z + stage_yz + stage_zy
    for copy in sent:
        copy.wait_send()


N_COPIES = 4 + 12 + 3 + 2 + len(X_PEERS) + 4 * len(Y_PEERS) + 3 * len(Z_PEERS)


def finish(gq_in, gk_in, gg_in, gq_out, gk_out, gg_out, sem):
    pairs = [(gk_in, gk_out), (gg_in, gg_out)] + [(gq_in.at[h], gq_out.at[h]) for h in range(4)]
    copies = [pltpu.make_async_copy(a, b, sem.at[i]) for i, (a, b) in enumerate(pairs)]
    for copy in copies:
        copy.start()
    for copy in copies:
        copy.wait()


def body(queries, out_grad, latent_keys, kv_gain, query_groups):
    q_t = jnp.transpose(queries[0], (1, 2, 0))
    k_t = jnp.transpose(latent_keys[0], (1, 0))
    any_spec = pl.BlockSpec(memory_space=pl.ANY)
    vmem_spec = pl.BlockSpec(memory_space=pltpu.VMEM)
    ny, nz, nx = len(Y_PEERS), len(Z_PEERS), len(X_PEERS)
    given = (q_t, out_grad[0], k_t, kv_gain.reshape(4, 128), query_groups)
    given = [pltpu.with_memory_space_constraint(a, pltpu.HBM) for a in given]
    results = (
        jax.ShapeDtypeStruct((4, WIDTH, 128), BF16),
        jax.ShapeDtypeStruct((4, WIDTH), F32),
        jax.ShapeDtypeStruct((4, 128), F32),
    )
    gq, gk, gg = pl.pallas_call(
        kernel,
        out_shape=results,
        in_specs=[any_spec] * 5,
        out_specs=(vmem_spec,) * 3,
        scratch_shapes=[
            pltpu.VMEM((4, WIDTH, 256), BF16),
            pltpu.VMEM((128, 4, LATENT), BF16),
            pltpu.VMEM((128, 4, LATENT), F32),
            pltpu.VMEM((4, 256, LATENT), BF16),
            pltpu.VMEM((3, WIDTH, 128), BF16),
            pltpu.VMEM((3, 128, WIDTH), BF16),
            pltpu.VMEM((4, 384, 256), F32),
            pltpu.VMEM((4, 384, 256), F32),
            pltpu.VMEM((4, 384, 256), BF16),
            pltpu.VMEM((4, 384, 256), BF16),
            pltpu.VMEM((4, 8, 256), F32),
            pltpu.VMEM((4, 8, 256), F32),
            pltpu.VMEM((3, 128, COLS_Y), BF16),
            pltpu.VMEM((3, ZL, 48, 128), BF16),
            pltpu.VMEM((ny, 3, 16, COLS_Y), BF16),
            pltpu.VMEM((nz, 48, 128), BF16),
            pltpu.VMEM((3, ZL, 16, 128), F32),
            pltpu.VMEM((3, ZL, 16, 128), BF16),
            pltpu.VMEM((nz, 16, 128), BF16),
            pltpu.VMEM((Y, 8, 128), F32),
            pltpu.VMEM((ny, 8, 128), F32),
            pltpu.VMEM((8, 128), F32),
            pltpu.VMEM((nx, 8, 128), F32),
            pltpu.VMEM((8, 128), F32),
            pltpu.VMEM((ny, 8, 128), F32),
            pltpu.VMEM((8, 128), F32),
            pltpu.VMEM((nz, 8, 128), F32),
            pltpu.VMEM((2, WIDTH, 256), F32),
            pltpu.VMEM((2, WIDTH, 256), F32),
            pltpu.VMEM((2, WIDTH, 256), F32),
            pltpu.VMEM((4, 128), F32),
            pltpu.SMEM((1, 6), jnp.int32),
            pltpu.SemaphoreType.DMA((8,)),
            pltpu.SemaphoreType.DMA((N_COPIES,)),
            pltpu.SemaphoreType.DMA((N_COPIES,)),
        ],
        compiler_params=pltpu.CompilerParams(
            collective_id=0, has_side_effects=True, vmem_limit_bytes=48 * 2**20
        ),
        cost_estimate=pl.CostEstimate(
            flops=5 * 2 * 512 * 768 * 550, bytes_accessed=3 * 2**20, transcendentals=512 * 768
        ),
        name="mla_backward",
    )(*given)
    gq, gk, gg = pl.pallas_call(
        finish,
        out_shape=results,
        in_specs=[any_spec] * 3,
        out_specs=(any_spec,) * 3,
        scratch_shapes=[pltpu.SemaphoreType.DMA((6,))],
        name="results",
    )(gq, gk, gg)
    grad_queries = jnp.transpose(gq, (2, 0, 1))[None]
    return grad_queries, gk.reshape(1, 1, 4, WIDTH), gg.reshape(LATENT)


def solution(mesh):
    in_specs = (
        P("dp", "ctx", "exp", None),
        P("dp", "ctx", "exp", None),
        P("dp", "ctx", None),
        P(),
        P("dp", None),
    )
    out_specs = (P("dp", "ctx", "exp", None), P("dp", "ctx", "exp", None), P())
    return jax.shard_map(body, mesh=mesh, in_specs=in_specs, out_specs=out_specs, check_vma=False)
```

```python
import math

import jax
import jax.numpy as jnp
from jax import lax
from jax.experimental import pallas as pl
from jax.experimental.pallas import tpu as pltpu
from jax.sharding import PartitionSpec as P

LATENT = 512
WIDTH = 576
ROPE = WIDTH - LATENT
SCALE = (0.1 * math.log(40.0) + 1.0) ** 2 / math.sqrt(192.0)
MASKED = -1e30
MESH_ID = pl.DeviceIdType.MESH
F32 = jnp.float32
BF16 = jnp.bfloat16

X, Y, ZH, ZL, CORES = 4, 8, 3, 4, 2
QUARTER = WIDTH // 4
PIECES = ((0, 80), (80, 64))
Y_PEERS = (4, 3, 5, 2, 6, 1, 7)
Z_PEERS = (6, 5, 7, 4, 8, 3, 9, 2, 10, 1, 11)
Z_FAR = 5
X_PEERS = ((0, 1), (1, 0), (3, 0), (2, 0), (1, 1), (3, 1), (2, 1))
COLS_Y = 384
NT = (((1,), (1,)), ((), ()))
NN = (((1,), (0,)), ((), ()))


def dot(a, b, dims=NN):
    return lax.dot_general(a, b, dims, preferred_element_type=F32)


def kernel(
    q_hbm, do_hbm, kt_hbm, gain_hbm, groups_hbm,
    gq_ref, gk_ref, gg_ref,
    qp, do_raw, do_f32, dop, kt, kr, st, dpt, ds, pw,
    stat, stat_in, h1, h2, h3, h1_in, h2_in, h3_in, t1, h1b, h1b_in, t2, t2b, t2_in,
    ga, ga_in, gb, gb_in, gc, gc_in, dq, dq_in, dq_own, gain_ref, groups_ref,
    local_sem, send_sem, recv_sem,
):
    x = lax.axis_index("dp")
    ctx = lax.axis_index("ctx")
    exp = lax.axis_index("exp")
    zh, core = ctx // CORES, ctx % CORES
    y, zl = exp // ZL, exp % ZL

    def device(dx=0, dy=0, dz=0, dl=0, dc=0):
        z = (zh * ZL + (zl + dl) % ZL + dz) % (ZH * ZL)
        return (
            (x + dx) % X,
            (z // ZL) * CORES + (core + dc) % CORES,
            ((y + dy) % Y) * ZL + z % ZL,
        )

    count = [0]

    def remote(src, dst, **where):
        i = count[0]
        count[0] += 1
        return pltpu.make_async_remote_copy(
            src_ref=src, dst_ref=dst, send_sem=send_sem.at[i], recv_sem=recv_sem.at[i],
            device_id=device(**where), device_id_type=MESH_ID,
        )

    loads = [pltpu.make_async_copy(kt_hbm, kt.at[0], local_sem.at[0])]
    loads.append(pltpu.make_async_copy(do_hbm, do_raw, local_sem.at[1]))
    for h in range(4):
        loads.append(
            pltpu.make_async_copy(
                q_hbm.at[h], qp.at[h // 2, :, pl.ds((h % 2) * 128, 128)], local_sem.at[2 + h]
            )
        )
    tables = [
        pltpu.make_async_copy(gain_hbm, gain_ref, local_sem.at[6]),
        pltpu.make_async_copy(groups_hbm, groups_ref, local_sem.at[7]),
    ]
    loads[0].start()

    barrier = pltpu.get_barrier_semaphore()
    peers = [dict(dz=d) for d in (4, 8, 2, 10, 1, 11)]
    peers += [dict(dy=d) for d in (2, 6, 1, 7)]
    peers += [dict(dx=d) for d in (2, 1, 3)] + [dict(dc=1)]
    for peer in peers:
        pl.semaphore_signal(barrier, inc=1, device_id=device(**peer), device_id_type=MESH_ID)
    for copy in loads[1:] + tables:
        copy.start()
    loads[0].wait()
    pl.semaphore_wait(barrier, len(peers))

    p0 = (y % 4) * QUARTER
    first = {}
    for at, (off, rows) in enumerate(PIECES):
        for rel in (1, 2):
            part = pl.ds(pl.multiple_of(p0 + off, 16), rows)
            first[rel, at] = remote(kt.at[0, part], kt.at[rel, part], dz=(ZH - rel) * ZL)
            first[rel, at].start()

    for copy in loads[2:]:
        copy.wait()
    swap_q = remote(qp.at[pl.ds(0, 2)], qp.at[pl.ds(2, 2)], dc=1)
    swap_q.start()
    loads[1].wait()
    do_f32[...] = do_raw[...].astype(F32)
    for h in range(4):
        dop[h // 2, pl.ds((h % 2) * 128, 128), :] = do_f32[:, h, :].astype(BF16)
    swap_do = remote(dop.at[pl.ds(0, 2)], dop.at[pl.ds(2, 2)], dc=1)
    swap_do.start()

    second = []
    for at, (off, rows) in enumerate(PIECES):
        for rel in (1, 2):
            first[rel, at].wait_recv()
            part = pl.ds(pl.multiple_of(p0 + off, 16), rows)
            for dy in (1, Y - 1, 2 if at == 0 else Y - 2):
                copy = remote(kt.at[rel, part], kt.at[rel, part], dy=dy)
                copy.start()
                second.append(copy)

    swap_q.wait_recv()
    swap_do.wait_recv()
    for copy in tables:
        copy.wait()

    def keys_in(rel):
        for c in range(0, LATENT, 128):
            kr[rel, :, c : c + 128] = kt[rel, c : c + 128, :].astype(F32).T.astype(BF16)
        kr[rel, :, LATENT:] = kt[rel, LATENT:, :].astype(F32).T.astype(BF16)

    diff = lax.broadcasted_iota(jnp.int32, (128, 256), 0) - (
        lax.broadcasted_iota(jnp.int32, (128, 256), 1) & 127
    )
    group = (groups_ref[0, ctx], groups_ref[0, zh * CORES + 1 - core])

    parts = {}

    def score(start, groups):
        first_row = start * 128
        keys = kr[start : start + groups].reshape(groups * 128, WIDTH)
        for cc in range(4):
            raw = dot(keys, qp[cc]) * SCALE
            grad = dot(keys[:, :LATENT], dop[cc], NT)
            dpt[cc, first_row : first_row + groups * 128, :] = grad
            for g in range(groups):
                rel = start + g
                base = ((zh + rel) % ZH) * CORES + core
                visible = diff <= (group[cc // 2] - base) * 128
                s = jnp.where(visible, raw[g * 128 : g * 128 + 128], MASKED)
                dp = grad[g * 128 : g * 128 + 128]
                m = jnp.max(s, axis=0, keepdims=True)
                p = jnp.where(visible, jnp.exp(s - m), 0.0)
                st[cc, rel * 128 : rel * 128 + 128, :] = p
                parts[rel, cc] = (
                    m, jnp.sum(p, axis=0, keepdims=True), jnp.sum(p * dp, axis=0, keepdims=True)
                )

    keys_in(0)
    score(0, 1)
    for copy in second:
        copy.wait_recv()
    for rel in (1, 2):
        keys_in(rel)
    score(1, 2)

    for cc in range(4):
        m = jnp.maximum(jnp.maximum(parts[0, cc][0], parts[1, cc][0]), parts[2, cc][0])
        e = [jnp.exp(parts[rel, cc][0] - m) for rel in range(3)]
        stat[cc, 0:1, :] = m
        stat[cc, 1:2, :] = sum(parts[rel, cc][1] * e[rel] for rel in range(3))
        stat[cc, 2:3, :] = sum(parts[rel, cc][2] * e[rel] for rel in range(3))
        stat[cc, 3:8, :] = jnp.zeros((5, 256), F32)
    swap_stat = remote(stat, stat_in, dc=1)
    swap_stat.start()
    swap_stat.wait_recv()

    both = []
    for cc in range(4):
        other = (cc + 2) % 4
        m0, l0, w0 = stat[cc, 0:1, :], stat[cc, 1:2, :], stat[cc, 2:3, :]
        m1, l1, w1 = stat_in[other, 0:1, :], stat_in[other, 1:2, :], stat_in[other, 2:3, :]
        m = jnp.maximum(m0, m1)
        e0, e1 = jnp.exp(m0 - m), jnp.exp(m1 - m)
        inv = 1.0 / (l0 * e0 + l1 * e1)
        both.append((m, inv, (w0 * e0 + w1 * e1) * inv))

    def weigh(rel):
        rows = pl.ds(rel * 128, 128)
        for cc in range(4):
            m, inv, delta = both[cc]
            w = st[cc, rows, :] * (jnp.exp(parts[rel, cc][0] - m) * inv)
            pw[cc, rows, :] = w.astype(BF16)
            ds[cc, rows, :] = (w * (dpt[cc, rows, :] - delta)).astype(BF16)

    def picks(rows, wanted):
        out_row = lax.broadcasted_iota(jnp.int32, (rows, 128), 0)
        in_row = lax.broadcasted_iota(jnp.int32, (rows, 128), 1)
        return (in_row == wanted(out_row)).astype(BF16)

    by_z = picks(128, lambda o: ((o & 31) >> 2) * 16 + (o >> 5) * 4 + (o & 3))
    by_z_low = picks(64, lambda o: ((o & 15) >> 2) * 16 + (o >> 4) * 4 + (o & 3))
    by_z_high = picks(64, lambda o: (((o & 15) >> 2) + 4) * 16 + (o >> 4) * 4 + (o & 3))
    gain = jnp.zeros((1, LATENT), F32)

    def key_part(start, groups, gain):
        for rel in range(start, start + groups):
            weigh(rel)
        rows = pl.ds(start * 128, groups * 128)
        dk = dot(ds[0, rows, :], qp[0], NT)
        dv = dot(pw[0, rows, :], dop[0])
        for cc in range(1, 4):
            dk = dk + dot(ds[cc, rows, :], qp[cc], NT)
            dv = dv + dot(pw[cc, rows, :], dop[cc])
        dk = dk * SCALE
        dv = dk[:, :LATENT] + dv
        for g in range(groups):
            rel = start + g
            full = dv[g * 128 : g * 128 + 128]
            h1[rel] = full[:, :COLS_Y].astype(BF16)
            main = dot(by_z, full[:, COLS_Y:].astype(BF16)).astype(BF16)
            rope = dk[g * 128 : g * 128 + 128, LATENT:].astype(BF16)
            low = dot(by_z_low, rope)
            high = dot(by_z_high, rope)
            side = jnp.concatenate([low, high], axis=1).astype(BF16)
            for l in range(ZL):
                h2[rel, l, 0:32, :] = main[l * 32 : l * 32 + 32, :]
                h2[rel, l, 32:48, :] = side[l * 16 : l * 16 + 16, :]
            if rel == 0:
                for t in (1, 2):
                    near = dot(by_z, h1[0, :, t * 128 : t * 128 + 128]).astype(BF16)
                    for l in range(ZL):
                        h3[l, t * 32 - 32 : t * 32, :] = near[l * 32 : l * 32 + 32, :]
            keys = kr[rel, :, :LATENT].astype(F32)
            gain = gain + jnp.sum(full * keys, axis=0, keepdims=True)
        return gain

    def pack(row, ref):
        for t in range(4):
            ref[t : t + 1, :] = row[:, t * 128 : (t + 1) * 128]
        ref[4:8, :] = jnp.zeros((4, 128), F32)

    def y_rows(dy):
        return pl.ds(pl.multiple_of(((y + dy) % Y) * 16, 16), 16)

    def z_at(dz):
        z = (zh * ZL + zl + dz) % (ZH * ZL)
        return (z // ZL + ZH - zh) % ZH, z % ZL

    gain = key_part(1, 2, gain)
    stage_z = [remote(h2.at[z_at(d)], h2_in.at[i], dz=d) for i, d in enumerate(Z_PEERS)]
    stage_y = [
        remote(h1.at[pl.ds(1, 2), y_rows(d), :], h1_in.at[i, pl.ds(1, 2)], dy=d)
        for i, d in enumerate(Y_PEERS)
    ]
    for i, copy in enumerate(stage_y):
        copy.start()
        if i < Z_FAR:
            stage_z[i].start()
    gain = key_part(0, 1, gain)
    stage_l = [remote(h3.at[(zl + d) % ZL], h3_in.at[d - 1], dl=d) for d in (1, 2, 3)]
    last_y = [
        remote(h1.at[0, y_rows(d), pl.ds(0, 128)], h1_in.at[i, 0, :, pl.ds(0, 128)], dy=d)
        for i, d in enumerate(Y_PEERS)
    ]
    pack(gain, ga)
    gain_a = [remote(ga, ga_in.at[i], dx=d, dc=c) for i, (d, c) in enumerate(X_PEERS)]
    for copy in stage_z[Z_FAR:] + stage_l + last_y + gain_a:
        copy.start()
    stage_y = stage_y + last_y

    def query_part(cc):
        total = dot(kt[0], ds[cc, 0:128, :])
        for rel in (1, 2):
            total = total + dot(kt[rel], ds[cc, rel * 128 : rel * 128 + 128, :])
        return total * SCALE

    swap_dq = []
    for cc in (2, 3):
        dq[cc - 2] = query_part(cc)
        copy = remote(dq.at[cc - 2], dq_in.at[cc - 2], dc=1)
        copy.start()
        swap_dq.append(copy)

    for copy in gain_a:
        copy.wait_recv()
    total = ga[...]
    for i in range(len(X_PEERS)):
        total = total + ga_in[i]
    gb[...] = total
    gain_b = [remote(gb, gb_in.at[i], dy=d) for i, d in enumerate(Y_PEERS)]
    for copy in gain_b:
        copy.start()

    for cc in range(2):
        dq_own[cc] = query_part(cc)

    t1[...] = jnp.zeros_like(t1)
    for copy in stage_y:
        copy.wait_recv()
    for rel in range(3):
        tiles = 3 if rel else 1
        part = h1[rel, y_rows(0), : tiles * 128].astype(F32)
        for i in range(len(Y_PEERS)):
            part = part + h1_in[i, rel, :, : tiles * 128].astype(F32)
        for l in range(ZL):
            for t in range(tiles):
                t1[rel, l, t * 4 : t * 4 + 4, :] = part[l * 4 : l * 4 + 4, t * 128 : (t + 1) * 128]
    h1b[...] = t1[...].astype(BF16)
    stage_yz = [
        remote(h1b.at[z_at(d)], h1b_in.at[i], dz=d) for i, d in enumerate(Z_PEERS)
    ]
    for copy in stage_yz:
        copy.start()

    for copy in gain_b:
        copy.wait_recv()
    total = gb[...]
    for i in range(len(Y_PEERS)):
        total = total + gb_in[i]
    gc[...] = total
    gain_c = [remote(gc, gc_in.at[i], dz=d) for i, d in enumerate(Z_PEERS)]
    for copy in gain_c:
        copy.start()

    for copy in stage_z + stage_l:
        copy.wait_recv()
    part = h2[0, zl].astype(F32)
    for i in range(len(Z_PEERS)):
        part = part + h2_in[i].astype(F32)
    near = h3[zl].astype(F32)
    for i in range(ZL - 1):
        near = near + h3_in[i].astype(F32)
    for yy in range(Y):
        t2[yy, 0:4, :] = part[yy * 4 : yy * 4 + 4, :]
        t2[yy, 4:8, :] = part[32 + (yy % 4) * 4 : 36 + (yy % 4) * 4, :]
        t2[yy, 8:12, :] = near[yy * 4 : yy * 4 + 4, :]
        t2[yy, 12:16, :] = near[32 + yy * 4 : 36 + yy * 4, :]
    t2b[...] = t2[...].astype(BF16)
    stage_zy = [remote(t2b.at[(y + d) % Y], t2_in.at[i], dy=d) for i, d in enumerate(Y_PEERS)]
    for copy in stage_zy:
        copy.start()

    for cc in range(2):
        swap_dq[cc].wait_recv()
        full = (dq_own[cc] + dq_in[cc]).astype(BF16)
        gq_ref[cc * 2] = full[:, :128]
        gq_ref[cc * 2 + 1] = full[:, 128:]

    for copy in stage_zy:
        copy.wait_recv()
    late = t2[y]
    for i in range(len(Y_PEERS)):
        late = late + t2_in[i].astype(F32)
    gk_ref[:, COLS_Y:LATENT] = late[0:4, :]
    gk_ref[:, LATENT:] = jnp.where(y < Y // 2, late[4:8, :ROPE], late[4:8, ROPE:])
    for copy in stage_yz:
        copy.wait_recv()
    part = t1[0, zl]
    for i in range(len(Z_PEERS)):
        part = part + h1b_in[i].astype(F32)
    gk_ref[:, 0:128] = part[0:4, :]
    gk_ref[:, 128:256] = part[4:8, :] + late[8:12, :]
    gk_ref[:, 256:COLS_Y] = part[8:12, :] + late[12:16, :]
    for copy in gain_c:
        copy.wait_recv()
    total = gc[...]
    for i in range(len(Z_PEERS)):
        total = total + gc_in[i]
    gg_ref[...] = total[0:4, :] / gain_ref[...]

    sent = list(first.values()) + second + [swap_q, swap_do, swap_stat] + swap_dq
    sent += gain_a + gain_b + gain_c + stage_y + stage_z + stage_l + stage_yz + stage_zy
    for copy in sent:
        copy.wait_send()


N_COPIES = 4 + 12 + 3 + 2 + len(X_PEERS) + 4 * len(Y_PEERS) + 3 * len(Z_PEERS) + 3


def finish(gq_in, gk_in, gg_in, gq_out, gk_out, gg_out, sem):
    pairs = [(gk_in, gk_out), (gg_in, gg_out)] + [(gq_in.at[h], gq_out.at[h]) for h in range(4)]
    copies = [pltpu.make_async_copy(a, b, sem.at[i]) for i, (a, b) in enumerate(pairs)]
    for copy in copies:
        copy.start()
    for copy in copies:
        copy.wait()


def body(queries, out_grad, latent_keys, kv_gain, query_groups):
    q_t = jnp.transpose(queries[0], (1, 2, 0))
    k_t = jnp.transpose(latent_keys[0], (1, 0))
    any_spec = pl.BlockSpec(memory_space=pl.ANY)
    vmem_spec = pl.BlockSpec(memory_space=pltpu.VMEM)
    ny, nz, nx = len(Y_PEERS), len(Z_PEERS), len(X_PEERS)
    given = (q_t, out_grad[0], k_t, kv_gain.reshape(4, 128), query_groups)
    given = [pltpu.with_memory_space_constraint(a, pltpu.HBM) for a in given]
    results = (
        jax.ShapeDtypeStruct((4, WIDTH, 128), BF16),
        jax.ShapeDtypeStruct((4, WIDTH), F32),
        jax.ShapeDtypeStruct((4, 128), F32),
    )
    gq, gk, gg = pl.pallas_call(
        kernel,
        out_shape=results,
        in_specs=[any_spec] * 5,
        out_specs=(vmem_spec,) * 3,
        scratch_shapes=[
            pltpu.VMEM((4, WIDTH, 256), BF16),
            pltpu.VMEM((128, 4, LATENT), BF16),
            pltpu.VMEM((128, 4, LATENT), F32),
            pltpu.VMEM((4, 256, LATENT), BF16),
            pltpu.VMEM((3, WIDTH, 128), BF16),
            pltpu.VMEM((3, 128, WIDTH), BF16),
            pltpu.VMEM((4, 384, 256), F32),
            pltpu.VMEM((4, 384, 256), F32),
            pltpu.VMEM((4, 384, 256), BF16),
            pltpu.VMEM((4, 384, 256), BF16),
            pltpu.VMEM((4, 8, 256), F32),
            pltpu.VMEM((4, 8, 256), F32),
            pltpu.VMEM((3, 128, COLS_Y), BF16),
            pltpu.VMEM((3, ZL, 48, 128), BF16),
            pltpu.VMEM((ZL, 64, 128), BF16),
            pltpu.VMEM((ny, 3, 16, COLS_Y), BF16),
            pltpu.VMEM((nz, 48, 128), BF16),
            pltpu.VMEM((ZL - 1, 64, 128), BF16),
            pltpu.VMEM((3, ZL, 16, 128), F32),
            pltpu.VMEM((3, ZL, 16, 128), BF16),
            pltpu.VMEM((nz, 16, 128), BF16),
            pltpu.VMEM((Y, 16, 128), F32),
            pltpu.VMEM((Y, 16, 128), BF16),
            pltpu.VMEM((ny, 16, 128), BF16),
            pltpu.VMEM((8, 128), F32),
            pltpu.VMEM((nx, 8, 128), F32),
            pltpu.VMEM((8, 128), F32),
            pltpu.VMEM((ny, 8, 128), F32),
            pltpu.VMEM((8, 128), F32),
            pltpu.VMEM((nz, 8, 128), F32),
            pltpu.VMEM((2, WIDTH, 256), F32),
            pltpu.VMEM((2, WIDTH, 256), F32),
            pltpu.VMEM((2, WIDTH, 256), F32),
            pltpu.VMEM((4, 128), F32),
            pltpu.SMEM((1, 6), jnp.int32),
            pltpu.SemaphoreType.DMA((8,)),
            pltpu.SemaphoreType.DMA((N_COPIES,)),
            pltpu.SemaphoreType.DMA((N_COPIES,)),
        ],
        compiler_params=pltpu.CompilerParams(
            collective_id=0, has_side_effects=True, vmem_limit_bytes=48 * 2**20
        ),
        cost_estimate=pl.CostEstimate(
            flops=5 * 2 * 512 * 768 * 550, bytes_accessed=3 * 2**20, transcendentals=512 * 768
        ),
        name="mla_backward",
    )(*given)
    gq, gk, gg = pl.pallas_call(
        finish,
        out_shape=results,
        in_specs=[any_spec] * 3,
        out_specs=(any_spec,) * 3,
        scratch_shapes=[pltpu.SemaphoreType.DMA((6,))],
        compiler_params=pltpu.CompilerParams(vmem_limit_bytes=2**20),
        name="results",
    )(*(pltpu.with_memory_space_constraint(a, pltpu.VMEM) for a in (gq, gk, gg)))
    grad_queries = jnp.transpose(gq, (2, 0, 1))[None]
    return grad_queries, gk.reshape(1, 1, 4, WIDTH), gg.reshape(LATENT)


def solution(mesh):
    in_specs = (
        P("dp", "ctx", "exp", None),
        P("dp", "ctx", "exp", None),
        P("dp", "ctx", None),
        P(),
        P("dp", None),
    )
    out_specs = (P("dp", "ctx", "exp", None), P("dp", "ctx", "exp", None), P())
    return jax.shard_map(body, mesh=mesh, in_specs=in_specs, out_specs=out_specs, check_vma=False)
```

```python
import math

import jax
import jax.numpy as jnp
from jax import lax
from jax.experimental import pallas as pl
from jax.experimental.pallas import tpu as pltpu
from jax.sharding import PartitionSpec as P

LATENT = 512
WIDTH = 576
ROPE = WIDTH - LATENT
SCALE = (0.1 * math.log(40.0) + 1.0) ** 2 / math.sqrt(192.0)
MASKED = -1e30
MESH_ID = pl.DeviceIdType.MESH
F32 = jnp.float32
BF16 = jnp.bfloat16

X, Y, ZH, ZL, CORES = 4, 8, 3, 4, 2
QUARTER = WIDTH // 4
PIECES = ((0, 80), (80, 64))
Y_PEERS = (4, 3, 5, 2, 6, 1, 7)
Z_PEERS = (6, 5, 7, 4, 8, 3, 9, 2, 10, 1, 11)
Z_FAR = 5
OTHER_GROUPS = tuple((rel, d) for rel in (1, 2) for d in range(ZL))
X_PEERS = ((0, 1), (1, 0), (3, 0), (2, 0), (1, 1), (3, 1), (2, 1))
COLS_Y = 384
NT = (((1,), (1,)), ((), ()))
NN = (((1,), (0,)), ((), ()))


class Group:
    def __init__(self, copies, sent, received):
        self.copies, self.sent, self.received = copies, sent, received

    def start(self):
        for copy in self.copies:
            copy.start()

    def wait_send(self):
        self.sent.wait()

    def wait_recv(self):
        self.received.wait()


def dot(a, b, dims=NN):
    return lax.dot_general(a, b, dims, preferred_element_type=F32)


def kernel(
    q_hbm, do_hbm, kt_hbm, gain_hbm, groups_hbm,
    gq_ref, gk_ref, gg_ref,
    qp, do_raw, do_f32, dop, kt, kr, st, dpt, ds, pw,
    stat, stat_in, h1, h2, h3, h1_in, h2_in, h3_in, t1, h1b, h1b_in, t2, t2b, t2_in,
    ga, ga_in, gb, gb_in, gc, gc_in, dq, dq_in, dq_own, gain_ref, groups_ref,
    local_sem, send_sem, recv_sem,
):
    x = lax.axis_index("dp")
    ctx = lax.axis_index("ctx")
    exp = lax.axis_index("exp")
    zh, core = ctx // CORES, ctx % CORES
    y, zl = exp // ZL, exp % ZL

    def device(dx=0, dy=0, dz=0, dl=0, dc=0):
        z = (zh * ZL + (zl + dl) % ZL + dz) % (ZH * ZL)
        return (
            (x + dx) % X,
            (z // ZL) * CORES + (core + dc) % CORES,
            ((y + dy) % Y) * ZL + z % ZL,
        )

    count = [0]

    def take():
        count[0] += 1
        return count[0] - 1

    def remote(src, dst, at=None, **where):
        i = take() if at is None else at
        return pltpu.make_async_remote_copy(
            src_ref=src, dst_ref=dst, send_sem=send_sem.at[i], recv_sem=recv_sem.at[i],
            device_id=device(**where), device_id_type=MESH_ID,
        )

    def together(whole, moves):
        i = take()
        return Group(
            [remote(src, dst, at=i, **where) for src, dst, where in moves],
            pltpu.make_async_copy(whole, whole, send_sem.at[i]),
            pltpu.make_async_copy(whole, whole, recv_sem.at[i]),
        )

    loads = [pltpu.make_async_copy(kt_hbm, kt.at[0], local_sem.at[0])]
    loads.append(pltpu.make_async_copy(do_hbm, do_raw, local_sem.at[1]))
    for h in range(4):
        loads.append(
            pltpu.make_async_copy(
                q_hbm.at[h], qp.at[h // 2, :, pl.ds((h % 2) * 128, 128)], local_sem.at[2 + h]
            )
        )
    tables = [
        pltpu.make_async_copy(gain_hbm, gain_ref, local_sem.at[6]),
        pltpu.make_async_copy(groups_hbm, groups_ref, local_sem.at[7]),
    ]
    loads[0].start()

    barrier = pltpu.get_barrier_semaphore()
    peers = [dict(dz=d) for d in (4, 8, 2, 10, 1, 11)]
    peers += [dict(dy=d) for d in (2, 6, 1, 7)]
    peers += [dict(dx=d) for d in (2, 1, 3)] + [dict(dc=1)]
    for peer in peers:
        pl.semaphore_signal(barrier, inc=1, device_id=device(**peer), device_id_type=MESH_ID)
    for copy in loads[1:] + tables:
        copy.start()
    loads[0].wait()
    pl.semaphore_wait(barrier, len(peers))

    p0 = (y % 4) * QUARTER
    first = {}
    for at, (off, rows) in enumerate(PIECES):
        for rel in (1, 2):
            part = pl.ds(pl.multiple_of(p0 + off, 16), rows)
            first[rel, at] = remote(kt.at[0, part], kt.at[rel, part], dz=(ZH - rel) * ZL)
            first[rel, at].start()

    for copy in loads[2:]:
        copy.wait()
    swap_q = remote(qp.at[pl.ds(0, 2)], qp.at[pl.ds(2, 2)], dc=1)
    swap_q.start()
    loads[1].wait()
    do_f32[...] = do_raw[...].astype(F32)
    for h in range(4):
        dop[h // 2, pl.ds((h % 2) * 128, 128), :] = do_f32[:, h, :].astype(BF16)
    swap_do = remote(dop.at[pl.ds(0, 2)], dop.at[pl.ds(2, 2)], dc=1)
    swap_do.start()

    moves = []
    for at, (off, rows) in enumerate(PIECES):
        for rel in (1, 2):
            part = pl.ds(pl.multiple_of(p0 + off, 16), rows)
            for dy in (1, Y - 1, 2 if at == 0 else Y - 2):
                moves.append((kt.at[rel, part], kt.at[rel, part], dict(dy=dy)))
    second = together(kt.at[pl.ds(1, 2), pl.ds(0, 3 * QUARTER)], moves)
    ready = iter(second.copies)
    for at in range(len(PIECES)):
        for rel in (1, 2):
            first[rel, at].wait_recv()
            for _ in range(3):
                next(ready).start()

    swap_q.wait_recv()
    swap_do.wait_recv()
    for copy in tables:
        copy.wait()

    def keys_in(rel):
        for c in range(0, LATENT, 128):
            kr[rel, :, c : c + 128] = kt[rel, c : c + 128, :].astype(F32).T.astype(BF16)
        kr[rel, :, LATENT:] = kt[rel, LATENT:, :].astype(F32).T.astype(BF16)

    diff = lax.broadcasted_iota(jnp.int32, (128, 256), 0) - (
        lax.broadcasted_iota(jnp.int32, (128, 256), 1) & 127
    )
    group = (groups_ref[0, ctx], groups_ref[0, zh * CORES + 1 - core])

    parts = {}

    def score(start, groups):
        first_row = start * 128
        keys = kr[start : start + groups].reshape(groups * 128, WIDTH)
        for cc in range(4):
            raw = dot(keys, qp[cc]) * SCALE
            grad = dot(keys[:, :LATENT], dop[cc], NT)
            dpt[cc, first_row : first_row + groups * 128, :] = grad
            for g in range(groups):
                rel = start + g
                base = ((zh + rel) % ZH) * CORES + core
                visible = diff <= (group[cc // 2] - base) * 128
                s = jnp.where(visible, raw[g * 128 : g * 128 + 128], MASKED)
                dp = grad[g * 128 : g * 128 + 128]
                m = jnp.max(s, axis=0, keepdims=True)
                p = jnp.where(visible, jnp.exp(s - m), 0.0)
                st[cc, rel * 128 : rel * 128 + 128, :] = p
                parts[rel, cc] = (
                    m, jnp.sum(p, axis=0, keepdims=True), jnp.sum(p * dp, axis=0, keepdims=True)
                )

    keys_in(0)
    score(0, 1)
    second.wait_recv()
    for rel in (1, 2):
        keys_in(rel)
    score(1, 2)

    for cc in range(4):
        m = jnp.maximum(jnp.maximum(parts[0, cc][0], parts[1, cc][0]), parts[2, cc][0])
        e = [jnp.exp(parts[rel, cc][0] - m) for rel in range(3)]
        stat[cc, 0:1, :] = m
        stat[cc, 1:2, :] = sum(parts[rel, cc][1] * e[rel] for rel in range(3))
        stat[cc, 2:3, :] = sum(parts[rel, cc][2] * e[rel] for rel in range(3))
        stat[cc, 3:8, :] = jnp.zeros((5, 256), F32)
    swap_stat = remote(stat, stat_in, dc=1)
    swap_stat.start()
    swap_stat.wait_recv()

    both = []
    for cc in range(4):
        other = (cc + 2) % 4
        m0, l0, w0 = stat[cc, 0:1, :], stat[cc, 1:2, :], stat[cc, 2:3, :]
        m1, l1, w1 = stat_in[other, 0:1, :], stat_in[other, 1:2, :], stat_in[other, 2:3, :]
        m = jnp.maximum(m0, m1)
        e0, e1 = jnp.exp(m0 - m), jnp.exp(m1 - m)
        inv = 1.0 / (l0 * e0 + l1 * e1)
        both.append((m, inv, (w0 * e0 + w1 * e1) * inv))

    def weigh(rel):
        rows = pl.ds(rel * 128, 128)
        for cc in range(4):
            m, inv, delta = both[cc]
            w = st[cc, rows, :] * (jnp.exp(parts[rel, cc][0] - m) * inv)
            pw[cc, rows, :] = w.astype(BF16)
            ds[cc, rows, :] = (w * (dpt[cc, rows, :] - delta)).astype(BF16)

    def picks(rows, wanted):
        out_row = lax.broadcasted_iota(jnp.int32, (rows, 128), 0)
        in_row = lax.broadcasted_iota(jnp.int32, (rows, 128), 1)
        return (in_row == wanted(out_row)).astype(BF16)

    by_z = picks(128, lambda o: ((o & 31) >> 2) * 16 + (o >> 5) * 4 + (o & 3))
    by_z_low = picks(64, lambda o: ((o & 15) >> 2) * 16 + (o >> 4) * 4 + (o & 3))
    by_z_high = picks(64, lambda o: (((o & 15) >> 2) + 4) * 16 + (o >> 4) * 4 + (o & 3))
    gain = jnp.zeros((1, LATENT), F32)

    def key_part(start, groups, gain):
        for rel in range(start, start + groups):
            weigh(rel)
        rows = pl.ds(start * 128, groups * 128)
        dk = dot(ds[0, rows, :], qp[0], NT)
        dv = dot(pw[0, rows, :], dop[0])
        for cc in range(1, 4):
            dk = dk + dot(ds[cc, rows, :], qp[cc], NT)
            dv = dv + dot(pw[cc, rows, :], dop[cc])
        dk = dk * SCALE
        dv = dk[:, :LATENT] + dv
        for g in range(groups):
            rel = start + g
            full = dv[g * 128 : g * 128 + 128]
            first_tiles = full[:, :COLS_Y].astype(BF16)
            if rel > 0:
                h1[rel - 1] = first_tiles
            else:
                for t in range(3):
                    near = dot(by_z, first_tiles[:, t * 128 : t * 128 + 128]).astype(BF16)
                    for l in range(ZL):
                        h3[l, t * 32 : t * 32 + 32, :] = near[l * 32 : l * 32 + 32, :]
            main = dot(by_z, full[:, COLS_Y:].astype(BF16)).astype(BF16)
            rope = dk[g * 128 : g * 128 + 128, LATENT:].astype(BF16)
            low = dot(by_z_low, rope)
            high = dot(by_z_high, rope)
            side = jnp.concatenate([low, high], axis=1).astype(BF16)
            for l in range(ZL):
                h2[rel, l, 0:32, :] = main[l * 32 : l * 32 + 32, :]
                h2[rel, l, 32:48, :] = side[l * 16 : l * 16 + 16, :]
            keys = kr[rel, :, :LATENT].astype(F32)
            gain = gain + jnp.sum(full * keys, axis=0, keepdims=True)
        return gain

    def pack(row, ref):
        for t in range(4):
            ref[t : t + 1, :] = row[:, t * 128 : (t + 1) * 128]
        ref[4:8, :] = jnp.zeros((4, 128), F32)

    def y_rows(dy):
        return pl.ds(pl.multiple_of(((y + dy) % Y) * 16, 16), 16)

    def z_at(dz):
        z = (zh * ZL + zl + dz) % (ZH * ZL)
        return (z // ZL + ZH - zh) % ZH, z % ZL

    gain = key_part(1, 2, gain)
    stage_z = together(
        h2_in, [(h2.at[z_at(d)], h2_in.at[i], dict(dz=d)) for i, d in enumerate(Z_PEERS)]
    )
    stage_y = together(
        h1_in, [(h1.at[:, y_rows(d), :], h1_in.at[i], dict(dy=d)) for i, d in enumerate(Y_PEERS)]
    )
    for i, copy in enumerate(stage_y.copies):
        copy.start()
        if i < Z_FAR:
            stage_z.copies[i].start()
    gain = key_part(0, 1, gain)
    stage_l = together(
        h3_in, [(h3.at[(zl + d) % ZL], h3_in.at[d - 1], dict(dl=d)) for d in (1, 2, 3)]
    )
    pack(gain, ga)
    gain_a = together(
        ga_in, [(ga, ga_in.at[i], dict(dx=d, dc=c)) for i, (d, c) in enumerate(X_PEERS)]
    )
    for copy in stage_z.copies[Z_FAR:] + stage_l.copies + gain_a.copies:
        copy.start()

    def query_part(cc):
        total = dot(kt[0], ds[cc, 0:128, :])
        for rel in (1, 2):
            total = total + dot(kt[rel], ds[cc, rel * 128 : rel * 128 + 128, :])
        return total * SCALE

    swap_dq = []
    for cc in (2, 3):
        dq[cc - 2] = query_part(cc)
        swap_dq.append(remote(dq.at[cc - 2], dq_in.at[cc - 2], dc=1))

    gain_a.wait_recv()
    total = ga[...]
    for i in range(len(X_PEERS)):
        total = total + ga_in[i]
    gb[...] = total
    gain_b = together(gb_in, [(gb, gb_in.at[i], dict(dy=d)) for i, d in enumerate(Y_PEERS)])
    for copy in gain_b.copies + swap_dq:
        copy.start()

    for cc in range(2):
        dq_own[cc] = query_part(cc)

    t1[...] = jnp.zeros_like(t1)
    t2[...] = jnp.zeros_like(t2)
    stage_y.wait_recv()
    for rel in range(2):
        part = h1[rel, y_rows(0), :].astype(F32)
        for i in range(len(Y_PEERS)):
            part = part + h1_in[i, rel].astype(F32)
        for l in range(ZL):
            for t in range(3):
                t1[rel, l, t * 4 : t * 4 + 4, :] = part[l * 4 : l * 4 + 4, t * 128 : (t + 1) * 128]
    h1b[...] = t1[...].astype(BF16)
    stage_yz = together(
        h1b_in,
        [
            (h1b.at[rel - 1, (zl + d) % ZL], h1b_in.at[i], dict(dz=rel * ZL, dl=d))
            for i, (rel, d) in enumerate(OTHER_GROUPS)
        ],
    )
    stage_yz.start()

    gain_b.wait_recv()
    total = gb[...]
    for i in range(len(Y_PEERS)):
        total = total + gb_in[i]
    gc[...] = total
    gain_c = together(gc_in, [(gc, gc_in.at[i], dict(dz=d)) for i, d in enumerate(Z_PEERS)])
    gain_c.start()

    stage_z.wait_recv()
    stage_l.wait_recv()
    part = h2[0, zl].astype(F32)
    for i in range(len(Z_PEERS)):
        part = part + h2_in[i].astype(F32)
    near = h3[zl].astype(F32)
    for i in range(ZL - 1):
        near = near + h3_in[i].astype(F32)
    for yy in range(Y):
        t2[yy, 0:4, :] = part[yy * 4 : yy * 4 + 4, :]
        t2[yy, 4:8, :] = part[32 + (yy % 4) * 4 : 36 + (yy % 4) * 4, :]
        for t in range(3):
            t2[yy, 8 + t * 4 : 12 + t * 4, :] = near[t * 32 + yy * 4 : t * 32 + yy * 4 + 4, :]
    t2b[...] = t2[...].astype(BF16)
    stage_zy = together(
        t2_in, [(t2b.at[(y + d) % Y], t2_in.at[i], dict(dy=d)) for i, d in enumerate(Y_PEERS)]
    )
    stage_zy.start()

    for cc in range(2):
        swap_dq[cc].wait_recv()
        full = (dq_own[cc] + dq_in[cc]).astype(BF16)
        gq_ref[cc * 2] = full[:, :128]
        gq_ref[cc * 2 + 1] = full[:, 128:]

    sent = list(first.values()) + [second, swap_q, swap_do, swap_stat] + swap_dq
    sent += [stage_y, stage_z, stage_l, stage_yz, stage_zy, gain_a, gain_b, gain_c]
    for copies in sent:
        copies.wait_send()

    stage_zy.wait_recv()
    late = t2[y]
    for i in range(len(Y_PEERS)):
        late = late + t2_in[i].astype(F32)
    gk_ref[:, COLS_Y:LATENT] = late[0:4, :]
    gk_ref[:, LATENT:] = jnp.where(y < Y // 2, late[4:8, :ROPE], late[4:8, ROPE:])
    stage_yz.wait_recv()
    part = late[8:20, :]
    for i in range(len(OTHER_GROUPS)):
        part = part + h1b_in[i, 0:12, :].astype(F32)
    for t in range(3):
        gk_ref[:, t * 128 : (t + 1) * 128] = part[t * 4 : t * 4 + 4, :]
    gain_c.wait_recv()
    total = gc[...]
    for i in range(len(Z_PEERS)):
        total = total + gc_in[i]
    gg_ref[...] = total[0:4, :] / gain_ref[...]


N_COPIES = 4 + 5 + 9


def finish(gq_in, gk_in, gg_in, gq_out, gk_out, gg_out, sem):
    pairs = [(gk_in, gk_out), (gg_in, gg_out)] + [(gq_in.at[h], gq_out.at[h]) for h in range(4)]
    copies = [pltpu.make_async_copy(a, b, sem.at[i]) for i, (a, b) in enumerate(pairs)]
    for copy in copies:
        copy.start()
    for copy in copies:
        copy.wait()


def body(queries, out_grad, latent_keys, kv_gain, query_groups):
    q_t = jnp.transpose(queries[0], (1, 2, 0))
    k_t = jnp.transpose(latent_keys[0], (1, 0))
    any_spec = pl.BlockSpec(memory_space=pl.ANY)
    vmem_spec = pl.BlockSpec(memory_space=pltpu.VMEM)
    ny, nz, nx = len(Y_PEERS), len(Z_PEERS), len(X_PEERS)
    given = (q_t, out_grad[0], k_t, kv_gain.reshape(4, 128), query_groups)
    given = [pltpu.with_memory_space_constraint(a, pltpu.HBM) for a in given]
    results = (
        jax.ShapeDtypeStruct((4, WIDTH, 128), BF16),
        jax.ShapeDtypeStruct((4, WIDTH), F32),
        jax.ShapeDtypeStruct((4, 128), F32),
    )
    gq, gk, gg = pl.pallas_call(
        kernel,
        out_shape=results,
        in_specs=[any_spec] * 5,
        out_specs=(vmem_spec,) * 3,
        scratch_shapes=[
            pltpu.VMEM((4, WIDTH, 256), BF16),
            pltpu.VMEM((128, 4, LATENT), BF16),
            pltpu.VMEM((128, 4, LATENT), F32),
            pltpu.VMEM((4, 256, LATENT), BF16),
            pltpu.VMEM((3, WIDTH, 128), BF16),
            pltpu.VMEM((3, 128, WIDTH), BF16),
            pltpu.VMEM((4, 384, 256), F32),
            pltpu.VMEM((4, 384, 256), F32),
            pltpu.VMEM((4, 384, 256), BF16),
            pltpu.VMEM((4, 384, 256), BF16),
            pltpu.VMEM((4, 8, 256), F32),
            pltpu.VMEM((4, 8, 256), F32),
            pltpu.VMEM((2, 128, COLS_Y), BF16),
            pltpu.VMEM((3, ZL, 48, 128), BF16),
            pltpu.VMEM((ZL, 96, 128), BF16),
            pltpu.VMEM((ny, 2, 16, COLS_Y), BF16),
            pltpu.VMEM((nz, 48, 128), BF16),
            pltpu.VMEM((ZL - 1, 96, 128), BF16),
            pltpu.VMEM((2, ZL, 16, 128), F32),
            pltpu.VMEM((2, ZL, 16, 128), BF16),
            pltpu.VMEM((len(OTHER_GROUPS), 16, 128), BF16),
            pltpu.VMEM((Y, 32, 128), F32),
            pltpu.VMEM((Y, 32, 128), BF16),
            pltpu.VMEM((ny, 32, 128), BF16),
            pltpu.VMEM((8, 128), F32),
            pltpu.VMEM((nx, 8, 128), F32),
            pltpu.VMEM((8, 128), F32),
            pltpu.VMEM((ny, 8, 128), F32),
            pltpu.VMEM((8, 128), F32),
            pltpu.VMEM((nz, 8, 128), F32),
            pltpu.VMEM((2, WIDTH, 256), F32),
            pltpu.VMEM((2, WIDTH, 256), F32),
            pltpu.VMEM((2, WIDTH, 256), F32),
            pltpu.VMEM((4, 128), F32),
            pltpu.SMEM((1, 6), jnp.int32),
            pltpu.SemaphoreType.DMA((8,)),
            pltpu.SemaphoreType.DMA((N_COPIES,)),
            pltpu.SemaphoreType.DMA((N_COPIES,)),
        ],
        compiler_params=pltpu.CompilerParams(
            collective_id=0, has_side_effects=True, vmem_limit_bytes=48 * 2**20
        ),
        cost_estimate=pl.CostEstimate(
            flops=5 * 2 * 512 * 768 * 550, bytes_accessed=3 * 2**20, transcendentals=512 * 768
        ),
        name="mla_backward",
    )(*given)
    gq, gk, gg = pl.pallas_call(
        finish,
        out_shape=results,
        in_specs=[any_spec] * 3,
        out_specs=(any_spec,) * 3,
        scratch_shapes=[pltpu.SemaphoreType.DMA((6,))],
        compiler_params=pltpu.CompilerParams(vmem_limit_bytes=2**20),
        name="results",
    )(*(pltpu.with_memory_space_constraint(a, pltpu.VMEM) for a in (gq, gk, gg)))
    grad_queries = jnp.transpose(gq, (2, 0, 1))[None]
    return grad_queries, gk.reshape(1, 1, 4, WIDTH), gg.reshape(LATENT)


def solution(mesh):
    in_specs = (
        P("dp", "ctx", "exp", None),
        P("dp", "ctx", "exp", None),
        P("dp", "ctx", None),
        P(),
        P("dp", None),
    )
    out_specs = (P("dp", "ctx", "exp", None), P("dp", "ctx", "exp", None), P())
    return jax.shard_map(body, mesh=mesh, in_specs=in_specs, out_specs=out_specs, check_vma=False)
```

```python
import math

import jax
import jax.numpy as jnp
from jax import lax
from jax.experimental import pallas as pl
from jax.experimental.pallas import tpu as pltpu
from jax.sharding import PartitionSpec as P

LATENT = 512
WIDTH = 576
ROPE = WIDTH - LATENT
SCALE = (0.1 * math.log(40.0) + 1.0) ** 2 / math.sqrt(192.0)
MASKED = -1e30
MESH_ID = pl.DeviceIdType.MESH
F32 = jnp.float32
BF16 = jnp.bfloat16

X, Y, ZH, ZL, CORES = 4, 8, 3, 4, 2
QUARTER = WIDTH // 4
PIECES = ((0, 80), (80, 64))
Y_PEERS = (4, 3, 5, 2, 6, 1, 7)
Z_PEERS = (6, 5, 7, 4, 8, 3, 9, 2, 10, 1, 11)
OTHER_GROUPS = tuple((rel, d) for rel in (1, 2) for d in range(ZL))
X_PEERS = ((0, 1), (1, 0), (3, 0), (2, 0), (1, 1), (3, 1), (2, 1))
COLS_Y = 384
NT = (((1,), (1,)), ((), ()))
NN = (((1,), (0,)), ((), ()))


class Group:
    def __init__(self, copies, sent, received):
        self.copies, self.sent, self.received = copies, sent, received

    def start(self):
        for copy in self.copies:
            copy.start()

    def wait_send(self):
        self.sent.wait()

    def wait_recv(self):
        self.received.wait()


def dot(a, b, dims=NN):
    return lax.dot_general(a, b, dims, preferred_element_type=F32)


def kernel(
    q_hbm, do_hbm, kt_hbm, gain_hbm, groups_hbm,
    gq_ref, gk_ref, gg_ref,
    qp, do_raw, do_f32, dop, kt, kr, st, dpt, ds, pw,
    stat, stat_in, h1, h2, h3, h1_in, h2_in, h3_in, t1, h1b, h1b_in, t2, t2b, t2_in,
    ga, ga_in, gb, gb_in, gc, gc_in, dq, dq_in, dq_own, gain_ref, groups_ref,
    local_sem, send_sem, recv_sem,
):
    x = lax.axis_index("dp")
    ctx = lax.axis_index("ctx")
    exp = lax.axis_index("exp")
    zh, core = ctx // CORES, ctx % CORES
    y, zl = exp // ZL, exp % ZL

    def device(dx=0, dy=0, dz=0, dl=0, dc=0):
        z = (zh * ZL + (zl + dl) % ZL + dz) % (ZH * ZL)
        return (
            (x + dx) % X,
            (z // ZL) * CORES + (core + dc) % CORES,
            ((y + dy) % Y) * ZL + z % ZL,
        )

    count = [0]

    def take():
        count[0] += 1
        return count[0] - 1

    def remote(src, dst, at=None, **where):
        i = take() if at is None else at
        return pltpu.make_async_remote_copy(
            src_ref=src, dst_ref=dst, send_sem=send_sem.at[i], recv_sem=recv_sem.at[i],
            device_id=device(**where), device_id_type=MESH_ID,
        )

    def together(whole, moves):
        i = take()
        return Group(
            [remote(src, dst, at=i, **where) for src, dst, where in moves],
            pltpu.make_async_copy(whole, whole, send_sem.at[i]),
            pltpu.make_async_copy(whole, whole, recv_sem.at[i]),
        )

    loads = [pltpu.make_async_copy(kt_hbm, kt.at[0], local_sem.at[0])]
    loads.append(pltpu.make_async_copy(do_hbm, do_raw, local_sem.at[1]))
    for h in range(4):
        loads.append(
            pltpu.make_async_copy(
                q_hbm.at[h], qp.at[h // 2, :, pl.ds((h % 2) * 128, 128)], local_sem.at[2 + h]
            )
        )
    tables = [
        pltpu.make_async_copy(gain_hbm, gain_ref, local_sem.at[6]),
        pltpu.make_async_copy(groups_hbm, groups_ref, local_sem.at[7]),
    ]
    loads[0].start()

    barrier = pltpu.get_barrier_semaphore()
    peers = [dict(dz=d) for d in (4, 8, 2, 10, 1, 11)]
    peers += [dict(dy=d) for d in (2, 6, 1, 7)]
    peers += [dict(dx=d) for d in (2, 1, 3)] + [dict(dc=1)]
    for peer in peers:
        pl.semaphore_signal(barrier, inc=1, device_id=device(**peer), device_id_type=MESH_ID)
    for copy in loads[1:] + tables:
        copy.start()
    loads[0].wait()
    pl.semaphore_wait(barrier, len(peers))

    p0 = (y % 4) * QUARTER
    first = {}
    for at, (off, rows) in enumerate(PIECES):
        for rel in (1, 2):
            part = pl.ds(pl.multiple_of(p0 + off, 16), rows)
            first[rel, at] = remote(kt.at[0, part], kt.at[rel, part], dz=(ZH - rel) * ZL)
            first[rel, at].start()

    for copy in loads[2:]:
        copy.wait()
    swap_q = remote(qp.at[pl.ds(0, 2)], qp.at[pl.ds(2, 2)], dc=1)
    swap_q.start()
    loads[1].wait()
    do_f32[...] = do_raw[...].astype(F32)
    for h in range(4):
        dop[h // 2, pl.ds((h % 2) * 128, 128), :] = do_f32[:, h, :].astype(BF16)
    swap_do = remote(dop.at[pl.ds(0, 2)], dop.at[pl.ds(2, 2)], dc=1)
    swap_do.start()

    moves = []
    for at, (off, rows) in enumerate(PIECES):
        for rel in (1, 2):
            part = pl.ds(pl.multiple_of(p0 + off, 16), rows)
            for dy in (1, Y - 1, 2 if at == 0 else Y - 2):
                moves.append((kt.at[rel, part], kt.at[rel, part], dict(dy=dy)))
    second = together(kt.at[pl.ds(1, 2), pl.ds(0, 3 * QUARTER)], moves)
    ready = iter(second.copies)
    for at in range(len(PIECES)):
        for rel in (1, 2):
            first[rel, at].wait_recv()
            for _ in range(3):
                next(ready).start()

    swap_q.wait_recv()
    swap_do.wait_recv()
    for copy in tables:
        copy.wait()

    def keys_in(rel):
        for c in range(0, LATENT, 128):
            kr[rel, :, c : c + 128] = kt[rel, c : c + 128, :].astype(F32).T.astype(BF16)
        kr[rel, :, LATENT:] = kt[rel, LATENT:, :].astype(F32).T.astype(BF16)

    diff = lax.broadcasted_iota(jnp.int32, (128, 256), 0) - (
        lax.broadcasted_iota(jnp.int32, (128, 256), 1) & 127
    )
    group = (groups_ref[0, ctx], groups_ref[0, zh * CORES + 1 - core])

    parts = {}

    def score(start, groups):
        first_row = start * 128
        keys = kr[start : start + groups].reshape(groups * 128, WIDTH)
        for cc in range(4):
            raw = dot(keys, qp[cc]) * SCALE
            grad = dot(keys[:, :LATENT], dop[cc], NT)
            dpt[cc, first_row : first_row + groups * 128, :] = grad
            for g in range(groups):
                rel = start + g
                base = ((zh + rel) % ZH) * CORES + core
                visible = diff <= (group[cc // 2] - base) * 128
                s = jnp.where(visible, raw[g * 128 : g * 128 + 128], MASKED)
                dp = grad[g * 128 : g * 128 + 128]
                m = jnp.max(s, axis=0, keepdims=True)
                p = jnp.where(visible, jnp.exp(s - m), 0.0)
                st[cc, rel * 128 : rel * 128 + 128, :] = p
                parts[rel, cc] = (
                    m, jnp.sum(p, axis=0, keepdims=True), jnp.sum(p * dp, axis=0, keepdims=True)
                )

    keys_in(0)
    score(0, 1)
    second.wait_recv()
    for rel in (1, 2):
        keys_in(rel)
    score(1, 2)

    for cc in range(4):
        m = jnp.maximum(jnp.maximum(parts[0, cc][0], parts[1, cc][0]), parts[2, cc][0])
        e = [jnp.exp(parts[rel, cc][0] - m) for rel in range(3)]
        stat[cc, 0:1, :] = m
        stat[cc, 1:2, :] = sum(parts[rel, cc][1] * e[rel] for rel in range(3))
        stat[cc, 2:3, :] = sum(parts[rel, cc][2] * e[rel] for rel in range(3))
        stat[cc, 3:8, :] = jnp.zeros((5, 256), F32)
    swap_stat = remote(stat, stat_in, dc=1)
    swap_stat.start()
    swap_stat.wait_recv()

    both = []
    for cc in range(4):
        other = (cc + 2) % 4
        m0, l0, w0 = stat[cc, 0:1, :], stat[cc, 1:2, :], stat[cc, 2:3, :]
        m1, l1, w1 = stat_in[other, 0:1, :], stat_in[other, 1:2, :], stat_in[other, 2:3, :]
        m = jnp.maximum(m0, m1)
        e0, e1 = jnp.exp(m0 - m), jnp.exp(m1 - m)
        inv = 1.0 / (l0 * e0 + l1 * e1)
        both.append((m, inv, (w0 * e0 + w1 * e1) * inv))

    def weigh(rel):
        rows = pl.ds(rel * 128, 128)
        for cc in range(4):
            m, inv, delta = both[cc]
            w = st[cc, rows, :] * (jnp.exp(parts[rel, cc][0] - m) * inv)
            pw[cc, rows, :] = w.astype(BF16)
            ds[cc, rows, :] = (w * (dpt[cc, rows, :] - delta)).astype(BF16)

    def picks(rows, wanted):
        out_row = lax.broadcasted_iota(jnp.int32, (rows, 128), 0)
        in_row = lax.broadcasted_iota(jnp.int32, (rows, 128), 1)
        return (in_row == wanted(out_row)).astype(BF16)

    by_z = picks(128, lambda o: ((o & 31) >> 2) * 16 + (o >> 5) * 4 + (o & 3))
    by_z_low = picks(64, lambda o: ((o & 15) >> 2) * 16 + (o >> 4) * 4 + (o & 3))
    by_z_high = picks(64, lambda o: (((o & 15) >> 2) + 4) * 16 + (o >> 4) * 4 + (o & 3))
    gain = jnp.zeros((1, LATENT), F32)

    def key_part(start, groups, gain):
        for rel in range(start, start + groups):
            weigh(rel)
        rows = pl.ds(start * 128, groups * 128)
        dk = dot(ds[0, rows, :], qp[0], NT)
        dv = dot(pw[0, rows, :], dop[0])
        for cc in range(1, 4):
            dk = dk + dot(ds[cc, rows, :], qp[cc], NT)
            dv = dv + dot(pw[cc, rows, :], dop[cc])
        dk = dk * SCALE
        dv = dk[:, :LATENT] + dv
        for g in range(groups):
            rel = start + g
            full = dv[g * 128 : g * 128 + 128]
            low_tiles = full[:, :COLS_Y].astype(BF16)
            main = dot(by_z, full[:, COLS_Y:].astype(BF16)).astype(BF16)
            rope = dk[g * 128 : g * 128 + 128, LATENT:].astype(BF16)
            low = dot(by_z_low, rope)
            high = dot(by_z_high, rope)
            side = jnp.concatenate([low, high], axis=1).astype(BF16)
            if rel > 0:
                h1[rel - 1] = low_tiles
            for l in range(ZL):
                to = h2.at[rel - 1, l] if rel > 0 else h3.at[l]
                to[0:32, :] = main[l * 32 : l * 32 + 32, :]
                to[32:48, :] = side[l * 16 : l * 16 + 16, :]
            if rel == 0:
                for t in range(3):
                    near = dot(by_z, low_tiles[:, t * 128 : t * 128 + 128]).astype(BF16)
                    for l in range(ZL):
                        h3[l, 48 + t * 32 : 80 + t * 32, :] = near[l * 32 : l * 32 + 32, :]
            keys = kr[rel, :, :LATENT].astype(F32)
            gain = gain + jnp.sum(full * keys, axis=0, keepdims=True)
        return gain

    def pack(row, ref):
        for t in range(4):
            ref[t : t + 1, :] = row[:, t * 128 : (t + 1) * 128]
        ref[4:8, :] = jnp.zeros((4, 128), F32)

    def y_rows(dy):
        return pl.ds(pl.multiple_of(((y + dy) % Y) * 16, 16), 16)

    gain = key_part(0, 3, gain)
    stage_z = together(
        h2_in,
        [
            (h2.at[rel - 1, (zl + d) % ZL], h2_in.at[i], dict(dz=rel * ZL, dl=d))
            for i, (rel, d) in enumerate(OTHER_GROUPS)
        ],
    )
    stage_y = together(
        h1_in, [(h1.at[:, y_rows(d), :], h1_in.at[i], dict(dy=d)) for i, d in enumerate(Y_PEERS)]
    )
    stage_l = together(
        h3_in, [(h3.at[(zl + d) % ZL], h3_in.at[d - 1], dict(dl=d)) for d in (1, 2, 3)]
    )
    pack(gain, ga)
    gain_a = together(
        ga_in, [(ga, ga_in.at[i], dict(dx=d, dc=c)) for i, (d, c) in enumerate(X_PEERS)]
    )
    for pair in zip(stage_z.copies, stage_y.copies):
        for copy in pair:
            copy.start()
    stage_z.copies[-1].start()
    gain_a.start()
    stage_l.start()

    def query_part(cc):
        total = dot(kt[0], ds[cc, 0:128, :])
        for rel in (1, 2):
            total = total + dot(kt[rel], ds[cc, rel * 128 : rel * 128 + 128, :])
        return total * SCALE

    swap_dq = []
    for cc in (2, 3):
        dq[cc - 2] = query_part(cc)
        swap_dq.append(remote(dq.at[cc - 2], dq_in.at[cc - 2], dc=1))

    gain_a.wait_recv()
    total = ga[...]
    for i in range(len(X_PEERS)):
        total = total + ga_in[i]
    gb[...] = total
    gain_b = together(gb_in, [(gb, gb_in.at[i], dict(dy=d)) for i, d in enumerate(Y_PEERS)])
    for copy in gain_b.copies + swap_dq:
        copy.start()

    for cc in range(2):
        dq_own[cc] = query_part(cc)

    t1[...] = jnp.zeros_like(t1)
    t2[...] = jnp.zeros_like(t2)
    stage_y.wait_recv()
    for rel in range(2):
        part = h1[rel, y_rows(0), :].astype(F32)
        for i in range(len(Y_PEERS)):
            part = part + h1_in[i, rel].astype(F32)
        for l in range(ZL):
            for t in range(3):
                t1[rel, l, t * 4 : t * 4 + 4, :] = part[l * 4 : l * 4 + 4, t * 128 : (t + 1) * 128]
    h1b[...] = t1[...].astype(BF16)
    stage_yz = together(
        h1b_in,
        [
            (h1b.at[rel - 1, (zl + d) % ZL], h1b_in.at[i], dict(dz=rel * ZL, dl=d))
            for i, (rel, d) in enumerate(OTHER_GROUPS)
        ],
    )
    stage_yz.start()

    gain_b.wait_recv()
    total = gb[...]
    for i in range(len(Y_PEERS)):
        total = total + gb_in[i]
    gc[...] = total
    gain_c = together(gc_in, [(gc, gc_in.at[i], dict(dz=d)) for i, d in enumerate(Z_PEERS)])
    gain_c.start()

    stage_z.wait_recv()
    stage_l.wait_recv()
    near = h3[zl].astype(F32)
    for i in range(ZL - 1):
        near = near + h3_in[i].astype(F32)
    part = near[0:48, :]
    for i in range(len(OTHER_GROUPS)):
        part = part + h2_in[i].astype(F32)
    for yy in range(Y):
        t2[yy, 0:4, :] = part[yy * 4 : yy * 4 + 4, :]
        t2[yy, 4:8, :] = part[32 + (yy % 4) * 4 : 36 + (yy % 4) * 4, :]
        for t in range(3):
            t2[yy, 8 + t * 4 : 12 + t * 4, :] = near[48 + t * 32 + yy * 4 : 52 + t * 32 + yy * 4, :]
    t2b[...] = t2[...].astype(BF16)
    stage_zy = together(
        t2_in, [(t2b.at[(y + d) % Y], t2_in.at[i], dict(dy=d)) for i, d in enumerate(Y_PEERS)]
    )
    stage_zy.start()

    for cc in range(2):
        swap_dq[cc].wait_recv()
        full = (dq_own[cc] + dq_in[cc]).astype(BF16)
        gq_ref[cc * 2] = full[:, :128]
        gq_ref[cc * 2 + 1] = full[:, 128:]

    sent = list(first.values()) + [second, swap_q, swap_do, swap_stat] + swap_dq
    sent += [stage_y, stage_z, stage_l, stage_yz, stage_zy, gain_a, gain_b, gain_c]
    for copies in sent:
        copies.wait_send()

    stage_zy.wait_recv()
    late = t2[y]
    for i in range(len(Y_PEERS)):
        late = late + t2_in[i].astype(F32)
    gk_ref[:, COLS_Y:LATENT] = late[0:4, :]
    gk_ref[:, LATENT:] = jnp.where(y < Y // 2, late[4:8, :ROPE], late[4:8, ROPE:])
    stage_yz.wait_recv()
    part = late[8:20, :]
    for i in range(len(OTHER_GROUPS)):
        part = part + h1b_in[i, 0:12, :].astype(F32)
    for t in range(3):
        gk_ref[:, t * 128 : (t + 1) * 128] = part[t * 4 : t * 4 + 4, :]
    gain_c.wait_recv()
    total = gc[...]
    for i in range(len(Z_PEERS)):
        total = total + gc_in[i]
    gg_ref[...] = total[0:4, :] / gain_ref[...]


N_COPIES = 4 + 5 + 9


def finish(gq_in, gk_in, gg_in, gq_out, gk_out, gg_out, sem):
    pairs = [(gk_in, gk_out), (gg_in, gg_out)] + [(gq_in.at[h], gq_out.at[h]) for h in range(4)]
    copies = [pltpu.make_async_copy(a, b, sem.at[i]) for i, (a, b) in enumerate(pairs)]
    for copy in copies:
        copy.start()
    for copy in copies:
        copy.wait()


def body(queries, out_grad, latent_keys, kv_gain, query_groups):
    q_t = jnp.transpose(queries[0], (1, 2, 0))
    k_t = jnp.transpose(latent_keys[0], (1, 0))
    any_spec = pl.BlockSpec(memory_space=pl.ANY)
    vmem_spec = pl.BlockSpec(memory_space=pltpu.VMEM)
    ny, nz, nx = len(Y_PEERS), len(Z_PEERS), len(X_PEERS)
    given = (q_t, out_grad[0], k_t, kv_gain.reshape(4, 128), query_groups)
    given = [pltpu.with_memory_space_constraint(a, pltpu.HBM) for a in given]
    results = (
        jax.ShapeDtypeStruct((4, WIDTH, 128), BF16),
        jax.ShapeDtypeStruct((4, WIDTH), F32),
        jax.ShapeDtypeStruct((4, 128), F32),
    )
    gq, gk, gg = pl.pallas_call(
        kernel,
        out_shape=results,
        in_specs=[any_spec] * 5,
        out_specs=(vmem_spec,) * 3,
        scratch_shapes=[
            pltpu.VMEM((4, WIDTH, 256), BF16),
            pltpu.VMEM((128, 4, LATENT), BF16),
            pltpu.VMEM((128, 4, LATENT), F32),
            pltpu.VMEM((4, 256, LATENT), BF16),
            pltpu.VMEM((3, WIDTH, 128), BF16),
            pltpu.VMEM((3, 128, WIDTH), BF16),
            pltpu.VMEM((4, 384, 256), F32),
            pltpu.VMEM((4, 384, 256), F32),
            pltpu.VMEM((4, 384, 256), BF16),
            pltpu.VMEM((4, 384, 256), BF16),
            pltpu.VMEM((4, 8, 256), F32),
            pltpu.VMEM((4, 8, 256), F32),
            pltpu.VMEM((2, 128, COLS_Y), BF16),
            pltpu.VMEM((2, ZL, 48, 128), BF16),
            pltpu.VMEM((ZL, 144, 128), BF16),
            pltpu.VMEM((ny, 2, 16, COLS_Y), BF16),
            pltpu.VMEM((len(OTHER_GROUPS), 48, 128), BF16),
            pltpu.VMEM((ZL - 1, 144, 128), BF16),
            pltpu.VMEM((2, ZL, 16, 128), F32),
            pltpu.VMEM((2, ZL, 16, 128), BF16),
            pltpu.VMEM((len(OTHER_GROUPS), 16, 128), BF16),
            pltpu.VMEM((Y, 32, 128), F32),
            pltpu.VMEM((Y, 32, 128), BF16),
            pltpu.VMEM((ny, 32, 128), BF16),
            pltpu.VMEM((8, 128), F32),
            pltpu.VMEM((nx, 8, 128), F32),
            pltpu.VMEM((8, 128), F32),
            pltpu.VMEM((ny, 8, 128), F32),
            pltpu.VMEM((8, 128), F32),
            pltpu.VMEM((nz, 8, 128), F32),
            pltpu.VMEM((2, WIDTH, 256), F32),
            pltpu.VMEM((2, WIDTH, 256), F32),
            pltpu.VMEM((2, WIDTH, 256), F32),
            pltpu.VMEM((4, 128), F32),
            pltpu.SMEM((1, 6), jnp.int32),
            pltpu.SemaphoreType.DMA((8,)),
            pltpu.SemaphoreType.DMA((N_COPIES,)),
            pltpu.SemaphoreType.DMA((N_COPIES,)),
        ],
        compiler_params=pltpu.CompilerParams(
            collective_id=0, has_side_effects=True, vmem_limit_bytes=48 * 2**20
        ),
        cost_estimate=pl.CostEstimate(
            flops=5 * 2 * 512 * 768 * 550, bytes_accessed=3 * 2**20, transcendentals=512 * 768
        ),
        name="mla_backward",
    )(*given)
    gq, gk, gg = pl.pallas_call(
        finish,
        out_shape=results,
        in_specs=[any_spec] * 3,
        out_specs=(any_spec,) * 3,
        scratch_shapes=[pltpu.SemaphoreType.DMA((6,))],
        compiler_params=pltpu.CompilerParams(vmem_limit_bytes=2**20),
        name="results",
    )(*(pltpu.with_memory_space_constraint(a, pltpu.VMEM) for a in (gq, gk, gg)))
    grad_queries = jnp.transpose(gq, (2, 0, 1))[None]
    return grad_queries, gk.reshape(1, 1, 4, WIDTH), gg.reshape(LATENT)


def solution(mesh):
    in_specs = (
        P("dp", "ctx", "exp", None),
        P("dp", "ctx", "exp", None),
        P("dp", "ctx", None),
        P(),
        P("dp", None),
    )
    out_specs = (P("dp", "ctx", "exp", None), P("dp", "ctx", "exp", None), P())
    return jax.shard_map(body, mesh=mesh, in_specs=in_specs, out_specs=out_specs, check_vma=False)
```

```python
import math

import jax
import jax.numpy as jnp
from jax import lax
from jax.experimental import pallas as pl
from jax.experimental.pallas import tpu as pltpu
from jax.sharding import PartitionSpec as P

LATENT = 512
WIDTH = 576
ROPE = WIDTH - LATENT
SCALE = (0.1 * math.log(40.0) + 1.0) ** 2 / math.sqrt(192.0)
MASKED = -1e30
MESH_ID = pl.DeviceIdType.MESH
F32 = jnp.float32
BF16 = jnp.bfloat16

X, Y, ZH, ZL, CORES = 4, 8, 3, 4, 2
QUARTER = WIDTH // 4
PIECES = ((0, 80), (80, 64))
Y_PEERS = (4, 3, 5, 2, 6, 1, 7)
Z_PEERS = (6, 5, 7, 4, 8, 3, 9, 2, 10, 1, 11)
OTHER_GROUPS = tuple((rel, d) for rel in (1, 2) for d in range(ZL))
X_PEERS = ((0, 1), (1, 0), (3, 0), (2, 0), (1, 1), (3, 1), (2, 1))
COLS_Y = 384
NT = (((1,), (1,)), ((), ()))
NN = (((1,), (0,)), ((), ()))


class Group:
    def __init__(self, copies, sent, received):
        self.copies, self.sent, self.received = copies, sent, received

    def start(self):
        for copy in self.copies:
            copy.start()

    def wait_send(self):
        self.sent.wait()

    def wait_recv(self):
        self.received.wait()


def dot(a, b, dims=NN):
    return lax.dot_general(a, b, dims, preferred_element_type=F32)


def kernel(
    q_hbm, do_hbm, kt_hbm, gain_hbm, groups_hbm,
    gq_ref, gk_ref, gg_ref,
    qp, do_raw, do_f32, dop, kt, kr, st, dpt, ds, pw,
    stat, stat_in, h1, h2, h3, h1_in, h2_in, h3_in, t1, h1b, h1b_in, t2, t2b, t2_in,
    ga, ga_in, gb, gb_in, gc, gc_in, dq, dq_in, dq_own, gain_ref, groups_ref,
    local_sem, send_sem, recv_sem,
):
    x = lax.axis_index("dp")
    ctx = lax.axis_index("ctx")
    exp = lax.axis_index("exp")
    zh, core = ctx // CORES, ctx % CORES
    y, zl = exp // ZL, exp % ZL

    def device(dx=0, dy=0, dz=0, dl=0, dc=0):
        z = (zh * ZL + (zl + dl) % ZL + dz) % (ZH * ZL)
        return (
            (x + dx) % X,
            (z // ZL) * CORES + (core + dc) % CORES,
            ((y + dy) % Y) * ZL + z % ZL,
        )

    count = [0]

    def take():
        count[0] += 1
        return count[0] - 1

    def remote(src, dst, at=None, **where):
        i = take() if at is None else at
        return pltpu.make_async_remote_copy(
            src_ref=src, dst_ref=dst, send_sem=send_sem.at[i], recv_sem=recv_sem.at[i],
            device_id=device(**where), device_id_type=MESH_ID,
        )

    def together(whole, moves):
        i = take()
        return Group(
            [remote(src, dst, at=i, **where) for src, dst, where in moves],
            pltpu.make_async_copy(whole, whole, send_sem.at[i]),
            pltpu.make_async_copy(whole, whole, recv_sem.at[i]),
        )

    loads = [pltpu.make_async_copy(kt_hbm, kt.at[0], local_sem.at[0])]
    loads.append(pltpu.make_async_copy(do_hbm, do_raw, local_sem.at[1]))
    for h in range(4):
        loads.append(
            pltpu.make_async_copy(
                q_hbm.at[h], qp.at[h // 2, :, pl.ds((h % 2) * 128, 128)], local_sem.at[2 + h]
            )
        )
    tables = [
        pltpu.make_async_copy(gain_hbm, gain_ref, local_sem.at[6]),
        pltpu.make_async_copy(groups_hbm, groups_ref, local_sem.at[7]),
    ]
    loads[0].start()

    barrier = pltpu.get_barrier_semaphore()
    peers = [dict(dz=d) for d in (4, 8, 2, 10, 1, 11)]
    peers += [dict(dy=d) for d in (2, 6, 1, 7)]
    peers += [dict(dx=d) for d in (2, 1, 3)] + [dict(dc=1)]
    for peer in peers:
        pl.semaphore_signal(barrier, inc=1, device_id=device(**peer), device_id_type=MESH_ID)
    for copy in loads[1:] + tables:
        copy.start()
    loads[0].wait()
    pl.semaphore_wait(barrier, len(peers))

    p0 = (y % 4) * QUARTER
    first = {}
    for at, (off, rows) in enumerate(PIECES):
        for rel in (1, 2):
            part = pl.ds(pl.multiple_of(p0 + off, 16), rows)
            first[rel, at] = remote(kt.at[0, part], kt.at[rel, part], dz=(ZH - rel) * ZL)
            first[rel, at].start()

    for copy in loads[2:]:
        copy.wait()
    swap_q = remote(qp.at[pl.ds(0, 2)], qp.at[pl.ds(2, 2)], dc=1)
    swap_q.start()
    loads[1].wait()
    do_f32[...] = do_raw[...].astype(F32)
    for h in range(4):
        dop[h // 2, pl.ds((h % 2) * 128, 128), :] = do_f32[:, h, :].astype(BF16)
    swap_do = remote(dop.at[pl.ds(0, 2)], dop.at[pl.ds(2, 2)], dc=1)
    swap_do.start()

    moves = []
    for at, (off, rows) in enumerate(PIECES):
        for rel in (1, 2):
            part = pl.ds(pl.multiple_of(p0 + off, 16), rows)
            for dy in (1, Y - 1, 2 if at == 0 else Y - 2):
                moves.append((kt.at[rel, part], kt.at[rel, part], dict(dy=dy)))
    second = together(kt.at[pl.ds(1, 2), pl.ds(0, 3 * QUARTER)], moves)
    ready = iter(second.copies)
    for at in range(len(PIECES)):
        for rel in (1, 2):
            first[rel, at].wait_recv()
            for _ in range(3):
                next(ready).start()

    swap_q.wait_recv()
    swap_do.wait_recv()
    for copy in tables:
        copy.wait()

    def keys_in(rel):
        for c in range(0, LATENT, 128):
            kr[rel, :, c : c + 128] = kt[rel, c : c + 128, :].astype(F32).T.astype(BF16)
        kr[rel, :, LATENT:] = kt[rel, LATENT:, :].astype(F32).T.astype(BF16)

    diff = lax.broadcasted_iota(jnp.int32, (128, 256), 0) - (
        lax.broadcasted_iota(jnp.int32, (128, 256), 1) & 127
    )
    group = (groups_ref[0, ctx], groups_ref[0, zh * CORES + 1 - core])

    parts = {}

    def score(start, groups):
        first_row = start * 128
        keys = kr[start : start + groups].reshape(groups * 128, WIDTH)
        for cc in range(4):
            raw = dot(keys, qp[cc]) * SCALE
            grad = dot(keys[:, :LATENT], dop[cc], NT)
            dpt[cc, first_row : first_row + groups * 128, :] = grad
            for g in range(groups):
                rel = start + g
                base = ((zh + rel) % ZH) * CORES + core
                visible = diff <= (group[cc // 2] - base) * 128
                s = jnp.where(visible, raw[g * 128 : g * 128 + 128], MASKED)
                dp = grad[g * 128 : g * 128 + 128]
                m = jnp.maximum(jnp.max(s, axis=0, keepdims=True), 0.1 * MASKED)
                p = jnp.exp(s - m)
                st[cc, rel * 128 : rel * 128 + 128, :] = p
                parts[rel, cc] = (
                    m, jnp.sum(p, axis=0, keepdims=True), jnp.sum(p * dp, axis=0, keepdims=True)
                )

    keys_in(0)
    score(0, 1)
    second.wait_recv()
    for rel in (1, 2):
        keys_in(rel)
    score(1, 2)

    for cc in range(4):
        m = jnp.maximum(jnp.maximum(parts[0, cc][0], parts[1, cc][0]), parts[2, cc][0])
        e = [jnp.exp(parts[rel, cc][0] - m) for rel in range(3)]
        stat[cc, 0:1, :] = m
        stat[cc, 1:2, :] = sum(parts[rel, cc][1] * e[rel] for rel in range(3))
        stat[cc, 2:3, :] = sum(parts[rel, cc][2] * e[rel] for rel in range(3))
        stat[cc, 3:8, :] = jnp.zeros((5, 256), F32)
    swap_stat = remote(stat, stat_in, dc=1)
    swap_stat.start()
    swap_stat.wait_recv()

    both = []
    for cc in range(4):
        other = (cc + 2) % 4
        m0, l0, w0 = stat[cc, 0:1, :], stat[cc, 1:2, :], stat[cc, 2:3, :]
        m1, l1, w1 = stat_in[other, 0:1, :], stat_in[other, 1:2, :], stat_in[other, 2:3, :]
        m = jnp.maximum(m0, m1)
        e0, e1 = jnp.exp(m0 - m), jnp.exp(m1 - m)
        inv = 1.0 / (l0 * e0 + l1 * e1)
        both.append((m, inv, (w0 * e0 + w1 * e1) * inv))

    def weigh(rel):
        rows = pl.ds(rel * 128, 128)
        for cc in range(4):
            m, inv, delta = both[cc]
            w = st[cc, rows, :] * (jnp.exp(parts[rel, cc][0] - m) * inv)
            pw[cc, rows, :] = w.astype(BF16)
            ds[cc, rows, :] = (w * (dpt[cc, rows, :] - delta)).astype(BF16)

    def picks(rows, wanted):
        out_row = lax.broadcasted_iota(jnp.int32, (rows, 128), 0)
        in_row = lax.broadcasted_iota(jnp.int32, (rows, 128), 1)
        return (in_row == wanted(out_row)).astype(BF16)

    by_z = picks(128, lambda o: ((o & 31) >> 2) * 16 + (o >> 5) * 4 + (o & 3))
    by_z_low = picks(64, lambda o: ((o & 15) >> 2) * 16 + (o >> 4) * 4 + (o & 3))
    by_z_high = picks(64, lambda o: (((o & 15) >> 2) + 4) * 16 + (o >> 4) * 4 + (o & 3))
    gain = jnp.zeros((1, LATENT), F32)

    def key_part(start, groups, gain):
        for rel in range(start, start + groups):
            weigh(rel)
        rows = pl.ds(start * 128, groups * 128)
        dk = dot(ds[0, rows, :], qp[0], NT)
        dv = dot(pw[0, rows, :], dop[0])
        for cc in range(1, 4):
            dk = dk + dot(ds[cc, rows, :], qp[cc], NT)
            dv = dv + dot(pw[cc, rows, :], dop[cc])
        dk = dk * SCALE
        dv = dk[:, :LATENT] + dv
        for g in range(groups):
            rel = start + g
            full = dv[g * 128 : g * 128 + 128]
            low_tiles = full[:, :COLS_Y].astype(BF16)
            main = dot(by_z, full[:, COLS_Y:].astype(BF16)).astype(BF16)
            rope = dk[g * 128 : g * 128 + 128, LATENT:].astype(BF16)
            low = dot(by_z_low, rope)
            high = dot(by_z_high, rope)
            side = jnp.concatenate([low, high], axis=1).astype(BF16)
            if rel > 0:
                h1[rel - 1] = low_tiles
            for l in range(ZL):
                to = h2.at[rel - 1, l] if rel > 0 else h3.at[l]
                to[0:32, :] = main[l * 32 : l * 32 + 32, :]
                to[32:48, :] = side[l * 16 : l * 16 + 16, :]
            if rel == 0:
                for t in range(3):
                    near = dot(by_z, low_tiles[:, t * 128 : t * 128 + 128]).astype(BF16)
                    for l in range(ZL):
                        h3[l, 48 + t * 32 : 80 + t * 32, :] = near[l * 32 : l * 32 + 32, :]
            keys = kr[rel, :, :LATENT].astype(F32)
            gain = gain + jnp.sum(full * keys, axis=0, keepdims=True)
        return gain

    def pack(row, ref):
        for t in range(4):
            ref[t : t + 1, :] = row[:, t * 128 : (t + 1) * 128]
        ref[4:8, :] = jnp.zeros((4, 128), F32)

    def y_rows(dy):
        return pl.ds(pl.multiple_of(((y + dy) % Y) * 16, 16), 16)

    gain = key_part(0, 3, gain)
    stage_z = together(
        h2_in,
        [
            (h2.at[rel - 1, (zl + d) % ZL], h2_in.at[i], dict(dz=rel * ZL, dl=d))
            for i, (rel, d) in enumerate(OTHER_GROUPS)
        ],
    )
    stage_y = together(
        h1_in, [(h1.at[:, y_rows(d), :], h1_in.at[i], dict(dy=d)) for i, d in enumerate(Y_PEERS)]
    )
    stage_l = together(
        h3_in, [(h3.at[(zl + d) % ZL], h3_in.at[d - 1], dict(dl=d)) for d in (1, 2, 3)]
    )
    pack(gain, ga)
    gain_a = together(
        ga_in, [(ga, ga_in.at[i], dict(dx=d, dc=c)) for i, (d, c) in enumerate(X_PEERS)]
    )
    for pair in zip(stage_z.copies, stage_y.copies):
        for copy in pair:
            copy.start()
    stage_z.copies[-1].start()
    gain_a.start()
    stage_l.start()

    def query_part(cc):
        total = dot(kt[0], ds[cc, 0:128, :])
        for rel in (1, 2):
            total = total + dot(kt[rel], ds[cc, rel * 128 : rel * 128 + 128, :])
        return total * SCALE

    swap_dq = []
    for cc in (2, 3):
        dq[cc - 2] = query_part(cc)
        swap_dq.append(remote(dq.at[cc - 2], dq_in.at[cc - 2], dc=1))

    gain_a.wait_recv()
    total = ga[...]
    for i in range(len(X_PEERS)):
        total = total + ga_in[i]
    gb[...] = total
    gain_b = together(gb_in, [(gb, gb_in.at[i], dict(dy=d)) for i, d in enumerate(Y_PEERS)])
    for copy in gain_b.copies + swap_dq:
        copy.start()

    for cc in range(2):
        dq_own[cc] = query_part(cc)

    t1[...] = jnp.zeros_like(t1)
    t2[...] = jnp.zeros_like(t2)
    stage_y.wait_recv()
    for rel in range(2):
        part = h1[rel, y_rows(0), :].astype(F32)
        for i in range(len(Y_PEERS)):
            part = part + h1_in[i, rel].astype(F32)
        for l in range(ZL):
            for t in range(3):
                t1[rel, l, t * 4 : t * 4 + 4, :] = part[l * 4 : l * 4 + 4, t * 128 : (t + 1) * 128]
    h1b[...] = t1[...].astype(BF16)
    stage_yz = together(
        h1b_in,
        [
            (h1b.at[rel - 1, (zl + d) % ZL], h1b_in.at[i], dict(dz=rel * ZL, dl=d))
            for i, (rel, d) in enumerate(OTHER_GROUPS)
        ],
    )
    stage_yz.start()

    gain_b.wait_recv()
    total = gb[...]
    for i in range(len(Y_PEERS)):
        total = total + gb_in[i]
    gc[...] = total
    gain_c = together(gc_in, [(gc, gc_in.at[i], dict(dz=d)) for i, d in enumerate(Z_PEERS)])
    gain_c.start()

    stage_z.wait_recv()
    stage_l.wait_recv()
    near = h3[zl].astype(F32)
    for i in range(ZL - 1):
        near = near + h3_in[i].astype(F32)
    part = near[0:48, :]
    for i in range(len(OTHER_GROUPS)):
        part = part + h2_in[i].astype(F32)
    for yy in range(Y):
        t2[yy, 0:4, :] = part[yy * 4 : yy * 4 + 4, :]
        t2[yy, 4:8, :] = part[32 + (yy % 4) * 4 : 36 + (yy % 4) * 4, :]
        for t in range(3):
            t2[yy, 8 + t * 4 : 12 + t * 4, :] = near[48 + t * 32 + yy * 4 : 52 + t * 32 + yy * 4, :]
    t2b[...] = t2[...].astype(BF16)
    stage_zy = together(
        t2_in, [(t2b.at[(y + d) % Y], t2_in.at[i], dict(dy=d)) for i, d in enumerate(Y_PEERS)]
    )
    stage_zy.start()

    for cc in range(2):
        swap_dq[cc].wait_recv()
        full = (dq_own[cc] + dq_in[cc]).astype(BF16)
        gq_ref[cc * 2] = full[:, :128]
        gq_ref[cc * 2 + 1] = full[:, 128:]

    sent = list(first.values()) + [second, swap_q, swap_do, swap_stat] + swap_dq
    sent += [stage_y, stage_z, stage_l, stage_yz, stage_zy, gain_a, gain_b, gain_c]
    for copies in sent:
        copies.wait_send()

    stage_zy.wait_recv()
    late = t2[y]
    for i in range(len(Y_PEERS)):
        late = late + t2_in[i].astype(F32)
    gk_ref[:, COLS_Y:LATENT] = late[0:4, :]
    gk_ref[:, LATENT:] = jnp.where(y < Y // 2, late[4:8, :ROPE], late[4:8, ROPE:])
    stage_yz.wait_recv()
    part = late[8:20, :]
    for i in range(len(OTHER_GROUPS)):
        part = part + h1b_in[i, 0:12, :].astype(F32)
    for t in range(3):
        gk_ref[:, t * 128 : (t + 1) * 128] = part[t * 4 : t * 4 + 4, :]
    gain_c.wait_recv()
    total = gc[...]
    for i in range(len(Z_PEERS)):
        total = total + gc_in[i]
    gg_ref[...] = total[0:4, :] / gain_ref[...]


N_COPIES = 4 + 5 + 9


def finish(gq_in, gk_in, gg_in, gq_out, gk_out, gg_out, sem):
    pairs = [(gk_in, gk_out), (gg_in, gg_out)] + [(gq_in.at[h], gq_out.at[h]) for h in range(4)]
    copies = [pltpu.make_async_copy(a, b, sem.at[i]) for i, (a, b) in enumerate(pairs)]
    for copy in copies:
        copy.start()
    for copy in copies:
        copy.wait()


def body(queries, out_grad, latent_keys, kv_gain, query_groups):
    q_t = jnp.transpose(queries[0], (1, 2, 0))
    k_t = jnp.transpose(latent_keys[0], (1, 0))
    any_spec = pl.BlockSpec(memory_space=pl.ANY)
    vmem_spec = pl.BlockSpec(memory_space=pltpu.VMEM)
    ny, nz, nx = len(Y_PEERS), len(Z_PEERS), len(X_PEERS)
    given = (q_t, out_grad[0], k_t, kv_gain.reshape(4, 128), query_groups)
    given = [pltpu.with_memory_space_constraint(a, pltpu.HBM) for a in given]
    results = (
        jax.ShapeDtypeStruct((4, WIDTH, 128), BF16),
        jax.ShapeDtypeStruct((4, WIDTH), F32),
        jax.ShapeDtypeStruct((4, 128), F32),
    )
    gq, gk, gg = pl.pallas_call(
        kernel,
        out_shape=results,
        in_specs=[any_spec] * 5,
        out_specs=(vmem_spec,) * 3,
        scratch_shapes=[
            pltpu.VMEM((4, WIDTH, 256), BF16),
            pltpu.VMEM((128, 4, LATENT), BF16),
            pltpu.VMEM((128, 4, LATENT), F32),
            pltpu.VMEM((4, 256, LATENT), BF16),
            pltpu.VMEM((3, WIDTH, 128), BF16),
            pltpu.VMEM((3, 128, WIDTH), BF16),
            pltpu.VMEM((4, 384, 256), F32),
            pltpu.VMEM((4, 384, 256), F32),
            pltpu.VMEM((4, 384, 256), BF16),
            pltpu.VMEM((4, 384, 256), BF16),
            pltpu.VMEM((4, 8, 256), F32),
            pltpu.VMEM((4, 8, 256), F32),
            pltpu.VMEM((2, 128, COLS_Y), BF16),
            pltpu.VMEM((2, ZL, 48, 128), BF16),
            pltpu.VMEM((ZL, 144, 128), BF16),
            pltpu.VMEM((ny, 2, 16, COLS_Y), BF16),
            pltpu.VMEM((len(OTHER_GROUPS), 48, 128), BF16),
            pltpu.VMEM((ZL - 1, 144, 128), BF16),
            pltpu.VMEM((2, ZL, 16, 128), F32),
            pltpu.VMEM((2, ZL, 16, 128), BF16),
            pltpu.VMEM((len(OTHER_GROUPS), 16, 128), BF16),
            pltpu.VMEM((Y, 32, 128), F32),
            pltpu.VMEM((Y, 32, 128), BF16),
            pltpu.VMEM((ny, 32, 128), BF16),
            pltpu.VMEM((8, 128), F32),
            pltpu.VMEM((nx, 8, 128), F32),
            pltpu.VMEM((8, 128), F32),
            pltpu.VMEM((ny, 8, 128), F32),
            pltpu.VMEM((8, 128), F32),
            pltpu.VMEM((nz, 8, 128), F32),
            pltpu.VMEM((2, WIDTH, 256), F32),
            pltpu.VMEM((2, WIDTH, 256), F32),
            pltpu.VMEM((2, WIDTH, 256), F32),
            pltpu.VMEM((4, 128), F32),
            pltpu.SMEM((1, 6), jnp.int32),
            pltpu.SemaphoreType.DMA((8,)),
            pltpu.SemaphoreType.DMA((N_COPIES,)),
            pltpu.SemaphoreType.DMA((N_COPIES,)),
        ],
        compiler_params=pltpu.CompilerParams(
            collective_id=0, has_side_effects=True, vmem_limit_bytes=48 * 2**20
        ),
        cost_estimate=pl.CostEstimate(
            flops=5 * 2 * 512 * 768 * 550, bytes_accessed=3 * 2**20, transcendentals=512 * 768
        ),
        name="mla_backward",
    )(*given)
    gq, gk, gg = pl.pallas_call(
        finish,
        out_shape=results,
        in_specs=[any_spec] * 3,
        out_specs=(any_spec,) * 3,
        scratch_shapes=[pltpu.SemaphoreType.DMA((6,))],
        compiler_params=pltpu.CompilerParams(vmem_limit_bytes=2**20),
        name="results",
    )(*(pltpu.with_memory_space_constraint(a, pltpu.VMEM) for a in (gq, gk, gg)))
    grad_queries = jnp.transpose(gq, (2, 0, 1))[None]
    return grad_queries, gk.reshape(1, 1, 4, WIDTH), gg.reshape(LATENT)


def solution(mesh):
    in_specs = (
        P("dp", "ctx", "exp", None),
        P("dp", "ctx", "exp", None),
        P("dp", "ctx", None),
        P(),
        P("dp", None),
    )
    out_specs = (P("dp", "ctx", "exp", None), P("dp", "ctx", "exp", None), P())
    return jax.shard_map(body, mesh=mesh, in_specs=in_specs, out_specs=out_specs, check_vma=False)
```
